128 devices in a mesh: layer: 8 (over y_hi, z), latent: 16 (over y_lo, x, core).
Axes of the slice: x: 4, y: 4 (y_hi: 2, y_lo: 2; y = y_hi * 2 + y_lo), z: 4, core: 2. Of those that a mesh axis runs over, the one named last changes fastest.
Arguments:
- acts: bfloat16 [8, 384, 2304], P('layer'), may hold values from -6 to 6
- decoder: bfloat16 [8, 32768, 2304], P('layer', 'latent'), may hold values from -0.225 to 0.225
- enc_bias: float32 [32768], P('latent'), may hold values from -3 to 3
- dec_bias: float32 [8, 2304], P('layer'), may hold values from -6 to 6
Outputs:
- grad_decoder: bfloat16 [8, 32768, 2304], P('layer', 'latent')
- grad_enc_bias: float32 [32768], P('latent')
- grad_dec_bias: float32 [8, 2304], P('layer')
- total_norm: float32 [32768], P('latent')
The draws below stay inside these ranges and needn't reach their ends.
All inputs are finite; a program needn't handle non-finite values.
Results may differ from the reference program's by a relative error of at most 0.03.
Values may be sent and summed in bfloat16 or wider, within the bound.
No kernel may reach another device: no remote copies, remote signals or barrier semaphores. Data moves between devices by JAX's collectives and lax.ppermute only.
A program may use at most 128 MiB of HBM per device.

```python
import math
import jax
import jax.numpy as jnp
from jax import lax

D = 2304
ROWS = 384
LAYERS = 8
F = 32768


def draw_decoder(key, part):
    key = jax.random.fold_in(key, 11)
    base_key, latent_key, feature_key = jax.random.split(key, 3)
    shape = (LAYERS, F, D)
    base = jnp.clip(jax.random.normal(base_key, shape, jnp.float32), -4.0, 4.0)
    steps = jnp.arange(LAYERS, dtype=jnp.float32) / max(LAYERS - 1, 1)
    layer_scale = 0.6 * jnp.exp(steps * math.log(3.0))
    latent_scale = jnp.exp(jax.random.uniform(latent_key, (LAYERS, F, 1), jnp.float32, math.log(0.5), math.log(2.0)))
    feature_scale = jnp.exp(jax.random.uniform(feature_key, (1, 1, D), jnp.float32, math.log(0.3), math.log(3.0)))
    values = base * layer_scale[:, None, None] * latent_scale * feature_scale / math.sqrt(2.0 * D * LAYERS)
    return values.astype(jnp.bfloat16)


def level_of(key, dims, cuts, smallest, top_value):
    def one(position, shards_of):
        draws = jax.random.uniform(jax.random.fold_in(jax.random.fold_in(key, 6), position), (shards_of,), jnp.float32, smallest / len(cuts), top_value / len(cuts))
        return jnp.repeat(jnp.exp(draws), dims[position] // shards_of).reshape((-1,) + (1,) * (len(dims) - position - 1))

    gain = one(*cuts[0])
    for cut in cuts[1:]:
        gain = gain * one(*cut)
    return gain


def gaussian(own_key, shape, deviation, reach, shards=(), kind=jnp.bfloat16):
    level = level_of(own_key, shape, shards, -0.22, 0.18) if shards else 1.0
    drawn = jax.random.normal(own_key, shape, jnp.float32) * deviation * level
    return jnp.minimum(jnp.maximum(drawn, -reach), reach).astype(kind)


def setup_inputs(seed: int = 0) -> dict:
    keys = jax.random.split(jax.random.key(seed), 5)
    return {
        "acts": gaussian(keys[0], (LAYERS, ROWS, D), 1.0, 6.0, ((0, 8),)),
        "decoder": draw_decoder(jax.random.fold_in(keys[4], 71), 0),
        "enc_bias": gaussian(keys[2], (F,), 0.5, 3.0, ((0, 16),), jnp.float32),
        "dec_bias": gaussian(keys[3], (LAYERS, D), 1.0, 6.0, ((0, 8),), jnp.float32),
    }


penalty_weight = 3.0
norm_eps = 1e-06

def rounded(value):
    return lax.optimization_barrier(value.astype(jnp.bfloat16)).astype(jnp.float32)

def reference(acts, decoder, enc_bias, dec_bias):
    high = lax.Precision.HIGHEST
    pre = jnp.zeros((ROWS, F), jnp.float32)
    totals = jnp.zeros((F,), jnp.float32)
    norm_list = []
    for layer in range(LAYERS):
        weights = decoder[layer].astype(jnp.float32)
        inputs = acts[layer].astype(jnp.float32)
        part = jnp.dot(inputs, weights.T, precision=high)
        pre = pre + rounded(part)
        norms = jnp.sqrt(lax.optimization_barrier(jnp.sum(weights * weights, axis=1)) + norm_eps)
        norm_list.append(norms)
        totals = totals + norms
    pre = pre + enc_bias[None, :]
    active = jnp.maximum(pre, 0.0)
    latents = active * active
    lat_round = rounded(latents)
    usage = lax.optimization_barrier(jnp.sum(latents, axis=0))
    scale = penalty_weight / ROWS
    dlat = jnp.zeros((ROWS, F), jnp.float32)
    error_list = []
    bias_list = []
    for layer in range(LAYERS):
        weights = decoder[layer].astype(jnp.float32)
        recon = jnp.dot(lat_round, weights, precision=high) + dec_bias[layer][None, :]
        err = recon - acts[layer].astype(jnp.float32)
        err_round = rounded(err * (2.0 / ROWS))
        error_list.append(err_round)
        bias_list.append(lax.optimization_barrier(jnp.sum(err_round, axis=0)))
        back = jnp.dot(err_round, weights.T, precision=high)
        dlat = dlat + rounded(back)
    dlat = dlat + scale * totals[None, :]
    dpre = dlat * (2.0 * active)
    grad_enc_bias = lax.optimization_barrier(jnp.sum(dpre, axis=0))
    dpre_round = rounded(dpre)
    grads = []
    for layer in range(LAYERS):
        weights = decoder[layer].astype(jnp.float32)
        inputs = acts[layer].astype(jnp.float32)
        grad = jnp.dot(lat_round.T, error_list[layer], precision=high)
        grad = grad + jnp.dot(dpre_round.T, inputs, precision=high)
        grad = grad + (scale * usage / norm_list[layer])[:, None] * weights
        grads.append(grad.astype(jnp.bfloat16))
    return (jnp.stack(grads), grad_enc_bias, jnp.stack(bias_list), totals)
```

```python
import jax
import jax.numpy as jnp
from jax import lax
from jax.experimental import pallas as pl
from jax.experimental.pallas import tpu as pltpu
from jax.sharding import PartitionSpec as P

penalty_weight = 3.0
norm_eps = 1e-06

D = 2304
ROWS = 384
F = 2048
LAYERS = 8
BLOCK = F // LAYERS
HALF = ROWS // 2
GROUP = 8
PIECE = HALF // GROUP
EXTRA = 16
SCALE = penalty_weight / ROWS

f32 = jnp.float32
bf16 = jnp.bfloat16
NT = (((1,), (1,)), ((), ()))
TN = (((0,), (0,)), ((), ()))
VMEM = pl.BlockSpec(memory_space=pltpu.VMEM)
HBM = pl.BlockSpec(memory_space=pltpu.HBM)
SMEM = pl.BlockSpec(memory_space=pltpu.SMEM)
shaped = jax.ShapeDtypeStruct


def call(kernel, operands, in_specs, out_specs, out_shape, scratch, mib, flops, nbytes, name):
    return pl.pallas_call(
        kernel,
        in_specs=in_specs,
        out_specs=out_specs,
        out_shape=out_shape,
        scratch_shapes=scratch,
        compiler_params=pltpu.CompilerParams(vmem_limit_bytes=mib << 20),
        cost_estimate=pl.CostEstimate(flops=flops, bytes_accessed=nbytes, transcendentals=0),
        name=name,
    )(*operands)


MATMUL = 2 * ROWS * F * D


def encode(core, acts, weights):
    parts = 4
    rows = F // parts

    def kernel(core_ref, a_hbm, w_hbm, out, norms, w, a, a_sem, w_sem):
        c = core_ref[0]
        a_copies = [
            pltpu.make_async_copy(
                a_hbm.at[pl.ds(pl.multiple_of(h * HALF, HALF), HALF)],
                a.at[pl.ds(i * HALF, HALF)],
                a_sem.at[i],
            )
            for i, h in enumerate((c, 1 - c))
        ]
        w_copies = [
            pltpu.make_async_copy(
                w_hbm.at[pl.ds(i * rows, rows)], w.at[pl.ds(i * rows, rows)], w_sem.at[i]
            )
            for i in range(parts)
        ]
        for copy in a_copies + w_copies:
            copy.start()
        for copy in a_copies:
            copy.wait()
        for i in range(parts):
            w_copies[i].wait()
            for j in range(i * rows // BLOCK, (i + 1) * rows // BLOCK):
                wb = w[pl.ds(j * BLOCK, BLOCK)]
                out[j, :ROWS] = lax.dot_general(
                    a[...], wb, NT, preferred_element_type=f32
                ).astype(bf16)
                squares = jnp.zeros((BLOCK, 128), f32)
                for k in range(D // 128):
                    x = wb[:, k * 128 : (k + 1) * 128].astype(f32)
                    squares = squares + x * x
                total = lax.dot_general(
                    jnp.ones((8, 128), f32),
                    squares,
                    NT,
                    precision=lax.Precision.HIGHEST,
                    preferred_element_type=f32,
                )
                norm = jnp.sqrt(total + norm_eps)
                norms[j] = norm
                high = norm.astype(bf16)
                low = (norm - high.astype(f32)).astype(bf16)
                out[j, ROWS:] = jnp.concatenate([high, low], axis=0)

    return call(
        kernel,
        (core, acts, weights),
        [SMEM, HBM, HBM],
        [VMEM] * 4,
        [
            shaped((LAYERS, ROWS + EXTRA, BLOCK), bf16),
            shaped((LAYERS, 8, BLOCK), f32),
            shaped((F, D), bf16),
            shaped((ROWS, D), bf16),
        ],
        [pltpu.SemaphoreType.DMA((2,)), pltpu.SemaphoreType.DMA((parts,))],
        46,
        MATMUL,
        F * D * 2,
        "encode",
    )


def activate(terms, bias):
    def kernel(t, b, out):
        pre = t[0, :ROWS].astype(f32)
        extra = t[0, ROWS:].astype(f32)
        for i in range(1, LAYERS):
            pre = pre + t[i, :ROWS].astype(f32)
            extra = extra + t[i, ROWS:].astype(f32)
        active = jnp.maximum(pre + b[...], 0.0).astype(bf16)
        total = extra[:8] + extra[8:]
        high = total.astype(bf16)
        low = (total - high.astype(f32)).astype(bf16)
        both = jnp.concatenate([high, low], axis=0)
        for i in range(LAYERS):
            out[i, :ROWS] = active
            out[i, ROWS:] = both

    return call(
        kernel,
        (terms, bias),
        [VMEM] * 2,
        VMEM,
        shaped((LAYERS, ROWS + EXTRA, BLOCK), bf16),
        [],
        8,
        2 * LAYERS * ROWS * BLOCK,
        2 * LAYERS * ROWS * BLOCK,
        "activate",
    )


def decode(active, weights):
    width = 256

    def kernel(g, w, lat, usage, total, recon, flat):
        for j in range(LAYERS):
            x = g[j, :ROWS].astype(f32)
            x = x * x
            usage[j] = jnp.broadcast_to(jnp.sum(x, axis=0, keepdims=True), (8, BLOCK))
            x = x.astype(bf16)
            lat[j] = x
            flat[:, j * BLOCK : (j + 1) * BLOCK] = x
            extra = g[j, ROWS:].astype(f32)
            total[j] = extra[:8] + extra[8:]
        for k in range(D // width):
            cols = slice(k * width, (k + 1) * width)
            recon[:, cols] = jnp.dot(
                flat[...], w[:, cols], preferred_element_type=f32
            ).astype(bf16)

    return call(
        kernel,
        (active, weights),
        [VMEM] * 2,
        [VMEM] * 4,
        [
            shaped((LAYERS, ROWS, BLOCK), bf16),
            shaped((LAYERS, 8, BLOCK), f32),
            shaped((LAYERS, 8, BLOCK), f32),
            shaped((ROWS, D), bf16),
        ],
        [pltpu.VMEM((ROWS, F), bf16)],
        24,
        MATMUL,
        2 * ROWS * F,
        "decode",
    )


def backward(errors, weights):
    def kernel(e, w, out, bias):
        x = e[...].astype(f32)
        bias[...] = jnp.broadcast_to(jnp.sum(x, axis=0, keepdims=True), (8, D))
        for j in range(LAYERS):
            out[j] = lax.dot_general(
                e[...], w[pl.ds(j * BLOCK, BLOCK)], NT, preferred_element_type=f32
            ).astype(bf16)

    return call(
        kernel,
        (errors, weights),
        [VMEM] * 2,
        [VMEM] * 2,
        [shaped((LAYERS, ROWS, BLOCK), bf16), shaped((8, D), f32)],
        [],
        24,
        MATMUL,
        2 * ROWS * F,
        "backward",
    )


def latent_grad(terms, active, total):
    def kernel(t, a, n, out):
        back = t[0].astype(f32)
        for i in range(1, LAYERS):
            back = back + t[i].astype(f32)
        back = back + SCALE * n[:1]
        dpre = (back * (2.0 * a[:ROWS].astype(f32))).astype(bf16)
        for i in range(LAYERS):
            out[i] = dpre

    return call(
        kernel,
        (terms, active, total),
        [VMEM] * 3,
        VMEM,
        shaped((LAYERS, ROWS, BLOCK), bf16),
        [],
        8,
        2 * LAYERS * ROWS * BLOCK,
        2 * LAYERS * ROWS * BLOCK,
        "latent_grad",
    )


def grad_first(lat, errors, usage, norms, weights):
    width = 768

    def kernel(l, e, u, n, w, out):
        for j in range(LAYERS):
            column = (SCALE * u[j] / n[j]).T[:, :1]
            rows = pl.ds(j * BLOCK, BLOCK)
            for k in range(D // width):
                cols = slice(k * width, (k + 1) * width)
                g = lax.dot_general(l[j], e[:, cols], TN, preferred_element_type=f32)
                out[rows, cols] = (g + column * w[rows, cols].astype(f32)).astype(bf16)

    return call(
        kernel,
        (lat, errors, usage, norms, weights),
        [VMEM] * 5,
        VMEM,
        shaped((F, D), bf16),
        [],
        28,
        MATMUL,
        2 * ROWS * F,
        "grad_first",
    )


def grad_second(dpre, acts, first):
    width = 768

    def kernel(d, a, f, out, bias, buf, sem):
        copies = []
        for j in range(LAYERS):
            bias[j] = jnp.broadcast_to(
                jnp.sum(d[j].astype(f32), axis=0, keepdims=True), (8, BLOCK)
            )
            if j >= 2:
                copies[j - 2].wait()
            rows = pl.ds(j * BLOCK, BLOCK)
            for k in range(D // width):
                cols = slice(k * width, (k + 1) * width)
                g = lax.dot_general(d[j], a[:, cols], TN, preferred_element_type=f32)
                buf[j % 2, :, cols] = (g + f[rows, cols].astype(f32)).astype(bf16)
            copy = pltpu.make_async_copy(buf.at[j % 2], out.at[rows], sem.at[j % 2])
            copy.start()
            copies.append(copy)
        copies[-2].wait()
        copies[-1].wait()

    return call(
        kernel,
        (dpre, acts, first),
        [VMEM] * 3,
        [HBM, VMEM],
        [shaped((F, D), bf16), shaped((LAYERS, 8, BLOCK), f32)],
        [pltpu.VMEM((2, BLOCK, D), bf16), pltpu.SemaphoreType.DMA((2,))],
        24,
        MATMUL,
        F * D * 2,
        "grad_second",
    )


def spread(x):
    return jnp.broadcast_to(x[None], (GROUP,) + x.shape)


def body(acts, decoder, enc_bias, dec_bias):
    inputs = acts[0]
    layer = lax.axis_index("layer")
    latent = lax.axis_index("latent")
    core = lax.rem(latent, 2)
    place = lax.div(latent, 2)
    groups = [[2 * g + c for g in range(GROUP)] for c in range(2)]
    swap = [(i, i ^ 1) for i in range(2 * GROUP)]

    def over_layers(x):
        return lax.all_to_all(x, "layer", 0, 0, tiled=True)

    def over_chips(x):
        return lax.all_to_all(x, "latent", 0, 0, axis_index_groups=groups, tiled=True)

    parts, norms, weights, rows = encode(
        jnp.reshape(core, (1,)).astype(jnp.int32), inputs, decoder[0]
    )
    bias = lax.dynamic_slice(enc_bias, (layer * BLOCK,), (BLOCK,))[None, :]
    mine = activate(over_layers(parts), bias)
    lat, usage, total, recon = decode(over_layers(mine), weights)

    other = lax.ppermute(recon[HALF:], "latent", swap)
    summed = (recon[:HALF].astype(f32) + other.astype(f32)).astype(bf16)
    pieces = over_chips(summed.reshape(GROUP, PIECE, D))
    own = lax.dynamic_slice(rows, (place * PIECE, 0), (PIECE, D))
    full = jnp.sum(pieces.astype(f32), axis=0) + dec_bias
    piece = ((full - own.astype(f32)) * (2.0 / ROWS)).astype(bf16)
    near = over_chips(spread(piece)).reshape(HALF, D)
    far = lax.ppermute(near, "latent", swap)
    errors = jnp.concatenate([near, far], axis=0)

    back, dec_grad = backward(errors, weights)
    my_total = lax.dynamic_index_in_dim(total, layer, 0, keepdims=False)
    dpre = over_layers(latent_grad(over_layers(back), mine[0], my_total))
    first = grad_first(lat, errors, usage, norms, weights)
    grad, enc_grad = grad_second(dpre, rows, first)
    return (
        grad[None],
        enc_grad[:, 0].reshape(F),
        dec_grad[:1],
        total[:, 0].reshape(F),
    )


def solution(mesh):
    placed = (P("layer", None, None), P("layer", "latent", None), P("latent"), P("layer", None))
    return jax.shard_map(
        body,
        mesh=mesh,
        in_specs=placed,
        out_specs=(P("layer", "latent", None), P("latent"), P("layer", None), P("latent")),
        check_vma=False,
    )
```

```python
import jax
import jax.numpy as jnp
from jax import lax
from jax.experimental import pallas as pl
from jax.experimental.pallas import tpu as pltpu
from jax.sharding import PartitionSpec as P

penalty_weight = 3.0
norm_eps = 1e-06

D = 2304
ROWS = 384
F = 2048
LAYERS = 8
BLOCK = F // LAYERS
EXTRA = 16
SCALE = penalty_weight / ROWS
MATMUL = 2 * ROWS * F * D

CHUNKS = ((0, 192, "z"), (192, 192, "z"))

f32 = jnp.float32
bf16 = jnp.bfloat16
NT = (((1,), (1,)), ((), ()))
TN = (((0,), (0,)), ((), ()))
VMEM = pl.BlockSpec(memory_space=pltpu.VMEM)
HBM = pl.BlockSpec(memory_space=pl.ANY)
SMEM = pl.BlockSpec(memory_space=pltpu.SMEM)


def half(*shape):
    return jax.ShapeDtypeStruct(shape, bf16)


def full(*shape):
    return jax.ShapeDtypeStruct(shape, f32)


def call(kernel, operands, out_shape, name, flops, scratch=(), mib=4, places=None, outs=None):
    many = isinstance(out_shape, (list, tuple))
    return pl.pallas_call(
        kernel,
        in_specs=places or [VMEM] * len(operands),
        out_specs=outs or ([VMEM] * len(out_shape) if many else VMEM),
        out_shape=out_shape,
        scratch_shapes=list(scratch),
        compiler_params=pltpu.CompilerParams(vmem_limit_bytes=mib << 20),
        cost_estimate=pl.CostEstimate(flops=flops, bytes_accessed=flops // 400, transcendentals=0),
        name=name,
    )(*operands)


def block(dy, dz):
    return dy * 4 + dz


def move_y(x):
    return lax.ppermute(x, "layer", [(i, i ^ 4) for i in range(8)])


def move_z(x, dz):
    return lax.ppermute(x, "layer", [(i, (i & 4) | ((i + dz) & 3)) for i in range(8)])


def move_core(x):
    return lax.ppermute(x, "latent", [(i, i ^ 1) for i in range(16)])


def move_x(x, dx):
    return lax.ppermute(x, "latent", [(i, (i & 9) | ((i + 2 * dx) & 6)) for i in range(16)])


def move_lo(x):
    return lax.ppermute(x, "latent", [(i, i ^ 8) for i in range(16)])


def split_sum(rows):
    return rows[:8].astype(f32) + rows[8:].astype(f32)


def split(value):
    high = value.astype(bf16)
    low = (value - high.astype(f32)).astype(bf16)
    return jnp.concatenate([high, low], axis=0)


def part_shapes(n, kind, extra):
    if kind == "z":
        return [half(2, n + extra, BLOCK)] * 4
    return [half(4, n, BLOCK)] * 2


def store_part(refs, kind, dy, dz, n, value):
    if kind == "z":
        refs[dz][dy, :n] = value
    else:
        refs[dy][dz, :n] = value


def encode(pos, acts, weights):
    shapes = []
    for i, (_, n, kind) in enumerate(CHUNKS):
        shapes += part_shapes(n, kind, EXTRA if i == 0 else 0)
    counts = [4 if kind == "z" else 2 for _, _, kind in CHUNKS]

    def kernel(pos_ref, acts_ref, w, *refs):
        groups, at = [], 0
        for count in counts:
            groups.append(refs[at : at + count])
            at += count
        norms, a = refs[at:]
        c = pos_ref[8]
        for start, n, _ in CHUNKS:
            h = n // 2
            for k, core in enumerate((c, 1 - c)):
                source = pl.multiple_of(start + core * h, 32)
                a[start + k * h : start + (k + 1) * h] = acts_ref[pl.ds(source, h)]
        for r in range(LAYERS):
            dy, dz = divmod(r, 4)
            wb = w[block_rows(pos_ref, r)]
            value = lax.dot_general(a[...], wb, NT, preferred_element_type=f32).astype(bf16)
            squares = jnp.zeros((BLOCK, 128), f32)
            for k in range(D // 128):
                x = wb[:, k * 128 : (k + 1) * 128].astype(f32)
                squares = squares + x * x
            total = lax.dot_general(
                jnp.ones((8, 128), f32),
                squares,
                NT,
                precision=lax.Precision.HIGHEST,
                preferred_element_type=f32,
            )
            norm = jnp.sqrt(total + norm_eps)
            norms[pos_ref[r]] = norm
            for i, (start, n, kind) in enumerate(CHUNKS):
                store_part(groups[i], kind, dy, dz, n, value[start : start + n])
                if i == 0:
                    groups[0][dz][dy, n:] = split(norm)

    out = call(
        kernel,
        (pos, acts, weights),
        shapes + [full(LAYERS, 8, BLOCK), half(ROWS, D)],
        "encode",
        MATMUL,
        (),
        24,
        [SMEM, VMEM, VMEM],
    )
    groups, at = [], 0
    for count in counts:
        groups.append(out[at : at + count])
        at += count
    return groups, out[at], out[at + 1]


def block_rows(pos_ref, r):
    return pl.ds(pl.multiple_of(pos_ref[r] * BLOCK, BLOCK), BLOCK)


def add_z(parts, extra):
    n = parts[0].shape[1] - extra

    def kernel(a, b, c, d, out):
        total = a[:, :n].astype(f32) + b[:, :n].astype(f32)
        total = total + (c[:, :n].astype(f32) + d[:, :n].astype(f32))
        out[:, :n] = total.astype(bf16)
        if extra:
            for k in range(2):
                out[k, n:] = split(sum(split_sum(x[k, n:]) for x in (a, b, c, d)))

    return call(kernel, parts, half(2, n + extra, BLOCK), "add_z", 1 << 20)


def add_y(own, other):
    n = own.shape[1]

    def kernel(a, b, *outs):
        for k in range(4):
            outs[k][...] = (a[k].astype(f32) + b[k].astype(f32)).astype(bf16)

    return call(kernel, (own, other), [half(n, BLOCK)] * 4, "add_y", 1 << 20)


def activate_z(pos, own, other, bias, extra):
    n = own.shape[1] - extra

    def kernel(pos_ref, a, b, bias_ref, out):
        for dy in range(2):
            pre = a[dy, :n].astype(f32) + b[1 - dy, :n].astype(f32)
            pre = pre + bias_ref[pos_ref[block(dy, 0)]]
            out[dy, :n] = jnp.maximum(pre, 0.0).astype(bf16)
            if extra:
                out[dy, n:] = split(split_sum(a[dy, n:]) + split_sum(b[1 - dy, n:]))

    return call(
        kernel,
        (pos, own, other, bias),
        half(2, n + extra, BLOCK),
        "activate_z",
        1 << 20,
        places=[SMEM, VMEM, VMEM, VMEM],
    )


def activate_y(pos, parts, bias):
    def kernel(pos_ref, a, b, c, d, bias_ref, out):
        pre = a[...].astype(f32) + b[...].astype(f32)
        pre = pre + (c[...].astype(f32) + d[...].astype(f32))
        out[...] = jnp.maximum(pre + bias_ref[pos_ref[0]], 0.0).astype(bf16)

    return call(
        kernel,
        (pos, *parts, bias),
        half(*parts[0].shape),
        "activate_y",
        1 << 20,
        places=[SMEM] + [VMEM] * 5,
    )


def stack(parts):
    def kernel(*refs):
        for k in range(4):
            refs[4][k] = refs[k][...]

    return call(kernel, parts, half(4, *parts[0].shape), "stack", 1 << 18)


def read_part(refs, kind, dy, dz):
    if kind == "z":
        return refs[dz][dy]
    return refs[dy][dz]


def decode(pos, active, kind, extra, weights):
    width = 768
    count = len(active)
    n = active[0].shape[1] - extra

    def kernel(pos_ref, *refs):
        g, w = refs[:count], refs[count]
        lat, mine, other = refs[count + 1 : count + 4]
        flat = refs[-1]
        for r in range(LAYERS):
            dy, dz = divmod(r, 4)
            part = read_part(g, kind, dy, dz)
            x = part[:n].astype(f32)
            lat[pos_ref[r]] = (x * x).astype(bf16)
            if extra:
                refs[count + 4][pos_ref[r]] = split_sum(part[n:])[:1]
        for j in range(LAYERS):
            flat[:, j * BLOCK : (j + 1) * BLOCK] = lat[j]
        for k in range(D // width):
            cols = slice(k * width, (k + 1) * width)
            value = jnp.dot(flat[...], w[:, cols], preferred_element_type=f32).astype(bf16)
            mine[:, cols] = value[: n // 2]
            other[:, cols] = value[n // 2 :]

    shapes = [half(LAYERS, n, BLOCK), half(n // 2, D), half(n // 2, D)]
    if extra:
        shapes.append(full(LAYERS, 1, BLOCK))
    return call(
        kernel,
        (pos, *active, weights),
        shapes,
        "decode",
        MATMUL * n // ROWS,
        [pltpu.VMEM((n, F), bf16)],
        20,
        [SMEM] + [VMEM] * (count + 1),
    )


def add_core(pos, own, other):
    n = own.shape[0] // 4

    def kernel(pos_ref, a, b, *refs):
        outs, held = refs[:4], refs[4]
        total = a[...].astype(f32) + b[...].astype(f32)
        for k in range(4):
            held[k] = total[k * n : (k + 1) * n].astype(bf16)
        for k in range(4):
            outs[k][...] = held[lax.rem(pos_ref[9] + k, 4)]

    return call(
        kernel,
        (pos, own, other),
        [half(n, D)] * 4,
        "add_core",
        1 << 20,
        [pltpu.VMEM((4, n, D), bf16)],
        places=[SMEM, VMEM, VMEM],
    )


def add_x(parts):
    def kernel(a, b, c, d, out):
        total = a[...].astype(f32) + b[...].astype(f32)
        out[...] = (total + (c[...].astype(f32) + d[...].astype(f32))).astype(bf16)

    return call(kernel, parts, half(*parts[0].shape), "add_x", 1 << 19)


def error(own, other, bias, acts):
    def kernel(a, b, bias_ref, x, out):
        value = a[...].astype(f32) + b[...].astype(f32) + bias_ref[...]
        out[...] = ((value - x[...].astype(f32)) * (2.0 / ROWS)).astype(bf16)

    return call(kernel, (own, other, bias, acts), half(*own.shape), "error", 1 << 19)


def join(pos, parts):
    n = parts[0].shape[0]

    def kernel(pos_ref, a, b, c, d, out, held):
        for k, piece in enumerate((a, b, c, d)):
            held[lax.rem(pos_ref[9] + 4 - k, 4)] = piece[...].astype(f32)
        out[...] = jnp.concatenate([held[k] for k in range(4)], axis=0).astype(bf16)

    return call(
        kernel,
        (pos, *parts),
        half(4 * n, D),
        "join",
        1 << 19,
        [pltpu.VMEM((4, n, D), f32)],
        places=[SMEM] + [VMEM] * 4,
    )


def backward(pos, near, far, kind, weights):
    n = 2 * near.shape[0]

    def kernel(pos_ref, a, b, w, *refs):
        e = refs[-1]
        e[: n // 2] = a[...]
        e[n // 2 :] = b[...]
        for r in range(LAYERS):
            value = lax.dot_general(
                e[...], w[block_rows(pos_ref, r)], NT, preferred_element_type=f32
            ).astype(bf16)
            store_part(refs, kind, *divmod(r, 4), n, value)

    out = call(
        kernel,
        (pos, near, far, weights),
        part_shapes(n, kind, 0) + [half(n, D)],
        "backward",
        MATMUL * n // ROWS,
        mib=20,
        places=[SMEM] + [VMEM] * 3,
    )
    return out[:-1], out[-1]


def latent_grad_z(pos, own, other, active, total):
    n = own.shape[1]

    def kernel(pos_ref, a, b, x, t, out):
        for dy in range(2):
            back = a[dy].astype(f32) + b[1 - dy].astype(f32) + SCALE * t[pos_ref[block(dy, 0)]]
            out[dy] = (back * (2.0 * x[dy, :n].astype(f32))).astype(bf16)

    return call(
        kernel,
        (pos, own, other, active, total),
        half(*own.shape),
        "latent_grad_z",
        1 << 20,
        places=[SMEM] + [VMEM] * 4,
    )


def latent_grad_y(pos, parts, active, total):
    def kernel(pos_ref, a, b, c, d, x, t, out):
        back = a[...].astype(f32) + b[...].astype(f32)
        back = back + (c[...].astype(f32) + d[...].astype(f32)) + SCALE * t[pos_ref[0]]
        out[...] = (back * (2.0 * x[...].astype(f32))).astype(bf16)

    return call(
        kernel,
        (pos, *parts, active, total),
        half(*parts[0].shape),
        "latent_grad_y",
        1 << 20,
        places=[SMEM] + [VMEM] * 6,
    )


def grad_first(lats, errors, norms, weights):
    width = 768
    count = len(lats)

    def kernel(*refs):
        ls, es = refs[:count], refs[count : 2 * count]
        n, w, out, bias, lhs, rhs = refs[2 * count :]
        sums = jnp.zeros((1, D), f32)
        for e, (start, rows, _) in zip(es, CHUNKS):
            rhs[start : start + rows] = e[...]
            sums = sums + jnp.sum(e[...].astype(f32), axis=0, keepdims=True)
        bias[...] = sums
        for j in range(LAYERS):
            for l, (start, rows, _) in zip(ls, CHUNKS):
                lhs[start : start + rows] = l[j]
            usage = jnp.sum(lhs[...].astype(f32), axis=0, keepdims=True)
            column = (SCALE * jnp.broadcast_to(usage, (8, BLOCK)) / n[j]).T[:, :1]
            rows = pl.ds(j * BLOCK, BLOCK)
            for k in range(D // width):
                cols = slice(k * width, (k + 1) * width)
                g = lax.dot_general(lhs[...], rhs[:, cols], TN, preferred_element_type=f32)
                out[rows, cols] = (g + column * w[rows, cols].astype(f32)).astype(bf16)

    return call(
        kernel,
        (*lats, *errors, norms, weights),
        [half(F, D), full(1, D)],
        "grad_first",
        MATMUL,
        [pltpu.VMEM((ROWS, BLOCK), bf16), pltpu.VMEM((ROWS, D), bf16)],
        26,
    )


def grad_second(pos, dpres, acts, first):
    width = 768
    steps = D // width
    counts = [len(d) for d in dpres]

    def kernel(pos_ref, *refs):
        groups, at = [], 0
        for count in counts:
            groups.append(refs[at : at + count])
            at += count
        a, f, out, bias, lhs, buf, sem = refs[at:]
        copies = []
        for r in range(LAYERS):
            dy, dz = divmod(r, 4)
            for g, (start, rows, kind) in zip(groups, CHUNKS):
                lhs[start : start + rows] = read_part(g, kind, dy, dz)
            bias[pos_ref[r]] = jnp.sum(lhs[...].astype(f32), axis=0, keepdims=True)
            rows = block_rows(pos_ref, r)
            slot = r % 4
            for k in range(steps):
                cols = slice(k * width, (k + 1) * width)
                g = lax.dot_general(lhs[...], a[:, cols], TN, preferred_element_type=f32)
                g = (g + f[rows, cols].astype(f32)).astype(bf16)
                if r >= 4:
                    copies[(r - 4) * steps + k].wait()
                buf[slot, :, cols] = g
                copy = pltpu.make_async_copy(
                    buf.at[slot, :, cols], out.at[rows, cols], sem.at[slot, k]
                )
                copy.start()
                copies.append(copy)
        for copy in copies[-4 * steps :]:
            copy.wait()

    flat = [x for d in dpres for x in d]
    return call(
        kernel,
        (pos, *flat, acts, first),
        [half(F, D), full(LAYERS, 1, BLOCK)],
        "grad_second",
        MATMUL,
        [
            pltpu.VMEM((ROWS, BLOCK), bf16),
            pltpu.VMEM((4, BLOCK, D), bf16),
            pltpu.SemaphoreType.DMA((4, steps)),
        ],
        20,
        [SMEM] + [VMEM] * (len(flat) + 2),
        [HBM, VMEM],
    )


def scatter_z(parts, extra=0):
    got = [move_z(parts[d], d) for d in (2, 1, 3)]
    own = add_z([parts[0]] + got, extra)
    return own, move_y(own)


def scatter_y(parts):
    pieces = add_y(parts[0], move_y(parts[1]))
    return [pieces[0]] + [move_z(pieces[d], d) for d in (2, 1, 3)]


def gather(own, kind):
    got = {d: move_z(own, 4 - d) for d in (2, 1, 3)}
    parts = [own, got[1], got[2], got[3]]
    if kind == "z":
        return parts
    both = stack(parts)
    return [both, move_y(both)]


def body(acts, decoder, enc_bias, dec_bias):
    inputs = acts[0]
    layer = lax.axis_index("layer")
    latent = lax.axis_index("latent")
    core, chip = latent & 1, (latent >> 1) & 3
    blocks = [
        ((layer // 4 + dy) % 2) * 4 + (layer % 4 + dz) % 4 for dy in range(2) for dz in range(4)
    ]
    pos = jnp.stack(blocks + [core, chip]).astype(jnp.int32)
    bias = enc_bias.reshape(LAYERS, 1, BLOCK)
    pieces = [
        lax.dynamic_slice(inputs, (start + core * (n // 2) + chip * (n // 8), 0), (n // 8, D))
        for start, n, _ in CHUNKS
    ]
    inputs, weights, pos, bias, dec_bias, pieces = lax.optimization_barrier(
        (inputs, decoder[0], pos, bias, dec_bias, pieces)
    )

    groups, norms, rows = encode(pos, inputs, weights)
    lats, errors, dpres = [], [], []
    total = None
    for i, (start, n, kind) in enumerate(CHUNKS):
        extra = EXTRA if i == 0 else 0
        if kind == "z":
            active = activate_z(pos, *scatter_z(groups[i], extra), bias, extra)
        else:
            active = activate_y(pos, scatter_y(groups[i]), bias)
        out = decode(pos, gather(active, kind), kind, extra, weights)
        lat, mine, other = out[:3]
        if extra:
            total = out[3]
        parts = add_core(pos, mine, move_core(other))
        own = add_x([parts[0]] + [move_x(parts[d], d) for d in (2, 1, 3)])
        piece = error(own, move_lo(own), dec_bias, pieces[i])
        got = {d: move_x(piece, d) for d in (2, 1, 3)}
        near = join(pos, [piece, got[1], got[2], got[3]])
        back, both = backward(pos, near, move_core(near), kind, weights)
        if kind == "z":
            dpre = latent_grad_z(pos, *scatter_z(back), active, total)
        else:
            dpre = latent_grad_y(pos, scatter_y(back), active, total)
        lats.append(lat)
        errors.append(both)
        dpres.append(gather(dpre, kind))
    first, dec_grad = grad_first(lats, errors, norms, weights)
    grad, enc_grad = grad_second(pos, dpres, rows, first)
    return grad[None], enc_grad.reshape(F), dec_grad, total.reshape(F)


def solution(mesh):
    placed = (P("layer", None, None), P("layer", "latent", None), P("latent"), P("layer", None))
    return jax.shard_map(
        body,
        mesh=mesh,
        in_specs=placed,
        out_specs=(P("layer", "latent", None), P("latent"), P("layer", None), P("latent")),
        check_vma=False,
    )
```

```python
import jax
import jax.numpy as jnp
from jax import lax
from jax.experimental import pallas as pl
from jax.experimental.pallas import tpu as pltpu
from jax.sharding import PartitionSpec as P

penalty_weight = 3.0
norm_eps = 1e-06

D = 2304
ROWS = 384
HALF = ROWS // 2
F = 2048
LAYERS = 8
BLOCK = F // LAYERS
CHIPS = 8
PIECE = HALF // CHIPS
EXTRA = 16
GROUPS = ((0, 4), (2, 1, 3), (6, 5, 7))
SCALE = penalty_weight / ROWS
MATMUL = 2 * ROWS * F * D

NEAR = (0, 1, 2, 3)
FAR = (4, 5, 6, 7)
STEPS = (2, 1, 3)

f32 = jnp.float32
bf16 = jnp.bfloat16
NT = (((1,), (1,)), ((), ()))
TN = (((0,), (0,)), ((), ()))
VMEM = pl.BlockSpec(memory_space=pltpu.VMEM)
HBM = pl.BlockSpec(memory_space=pl.ANY)


def half(*shape):
    return jax.ShapeDtypeStruct(shape, bf16)


def full(*shape):
    return jax.ShapeDtypeStruct(shape, f32)


def call(kernel, operands, out_shape, name, flops, scratch=(), mib=4, places=None, outs=None, aliases=None):
    many = isinstance(out_shape, (list, tuple))
    return pl.pallas_call(
        kernel,
        in_specs=places or [VMEM] * len(operands),
        out_specs=outs or ([VMEM] * len(out_shape) if many else VMEM),
        out_shape=out_shape,
        scratch_shapes=list(scratch),
        input_output_aliases=aliases or {},
        compiler_params=pltpu.CompilerParams(vmem_limit_bytes=mib << 20),
        cost_estimate=pl.CostEstimate(flops=flops, bytes_accessed=flops // 400, transcendentals=0),
        name=name,
    )(*operands)


def move_y(x):
    return lax.ppermute(x, "layer", [(i, i ^ 4) for i in range(8)])


def move_z(x, dz):
    return lax.ppermute(x, "layer", [(i, i & 4 | ((i + dz) & 3)) for i in range(8)])


def move_core(x):
    return lax.ppermute(x, "latent", [(i, i ^ 1) for i in range(16)])


def move_lo(x):
    return lax.ppermute(x, "latent", [(i, i ^ 8) for i in range(16)])


def move_x(x, dx):
    return lax.ppermute(x, "latent", [(i, i & 9 | ((i + 2 * dx) & 6)) for i in range(16)])


def near(index, r):
    dy, step = divmod(r, 4)
    return ((index & 4) ^ (4 * dy)) | ((index + step) & 3)


def block_of(r):
    return near(lax.axis_index("layer"), r)


def chip_of(r):
    return near(lax.axis_index("latent") >> 1, r)


def block_rows(r):
    return pl.ds(pl.multiple_of(block_of(r) * BLOCK, BLOCK), BLOCK)


def split_sum(rows):
    return rows[:8].astype(f32) + rows[8:].astype(f32)


def split(value):
    high = value.astype(bf16)
    low = (value - high.astype(f32)).astype(bf16)
    return jnp.concatenate([high, low], axis=0)


def product(rows, weights):
    return lax.dot_general(rows, weights, NT, preferred_element_type=f32).astype(bf16)


def encode_far(acts, weights):
    def kernel(a, w, *refs):
        rows = refs[4]
        c = lax.axis_index("latent") & 1
        for k, source in enumerate((c, 1 - c)):
            rows[k * HALF : (k + 1) * HALF] = a[pl.ds(pl.multiple_of(source * HALF, HALF), HALF)]
        for k, r in enumerate(FAR):
            refs[k][...] = product(rows[...], w[block_rows(r)])

    return call(
        kernel,
        (acts, weights),
        [half(ROWS, BLOCK)] * 4 + [half(ROWS, D)],
        "encode_far",
        MATMUL // 2,
        mib=8,
    )


def encode_near(rows, weights):
    def kernel(a, w, *outs):
        for k, r in enumerate(NEAR):
            outs[k][...] = product(a[...], w[block_rows(r)])

    return call(
        kernel, (rows, weights), [half(ROWS, BLOCK)] * 4, "encode_near", MATMUL // 2, mib=8
    )


def prepare(rows, weights):
    def kernel(a, w, norms, piece, held):
        for r in range(LAYERS):
            wb = w[block_rows(r)]
            squares = jnp.zeros((BLOCK, 128), f32)
            for i in range(D // 128):
                x = wb[:, i * 128 : (i + 1) * 128].astype(f32)
                squares = squares + x * x
            total = lax.dot_general(
                jnp.ones((8, 128), f32),
                squares,
                NT,
                precision=lax.Precision.HIGHEST,
                preferred_element_type=f32,
            )
            norms[r] = jnp.sqrt(total + norm_eps)
        value = a[:HALF].astype(f32)
        for k in range(CHIPS):
            held[k] = value[k * PIECE : (k + 1) * PIECE]
        piece[...] = held[chip_of(0)].astype(bf16)

    return call(
        kernel,
        (rows, weights),
        [full(LAYERS, 8, BLOCK), half(PIECE, D)],
        "prepare",
        1 << 30,
        [pltpu.VMEM((CHIPS, PIECE, D), f32)],
        8,
    )


def add(terms):
    value = terms[0][:ROWS].astype(f32)
    for x in terms[1:]:
        value = value + x[:ROWS].astype(f32)
    return value


def add_extra(terms):
    return sum(split_sum(x[ROWS:]) for x in terms)


def add_z(terms):
    extra = terms[0].shape[0] - ROWS

    def kernel(*refs):
        t, out = refs[:4], refs[4]
        out[:ROWS] = add(t).astype(bf16)
        if extra:
            out[ROWS:] = split(add_extra(t))

    return call(kernel, terms, half(*terms[0].shape), "add_z", 1 << 20)


def activate(terms, bias):
    def kernel(*refs):
        t, (b, out) = refs[:5], refs[5:]
        out[...] = jnp.maximum(add(t) + b[block_of(0)], 0.0).astype(bf16)

    return call(kernel, (*terms, bias), half(ROWS, BLOCK), "activate", 1 << 20)


def decode(active, weights, blocks, before=None, after=()):
    width = 768

    def kernel(*refs):
        g, w, refs = refs[:4], refs[4], refs[5:]
        if before is not None:
            acc, lat, mine, other = refs
        else:
            lat, out = refs[len(after) :]
        for k in range(4):
            x = g[k][...].astype(f32)
            lat[k] = (x * x).astype(bf16)
        for i in range(D // width):
            cols = slice(i * width, (i + 1) * width)
            value = None if before is None else acc[:, cols]
            for k, r in enumerate(blocks):
                term = jnp.dot(lat[k], w[block_rows(r), cols], preferred_element_type=f32)
                value = term if value is None else value + term
            if before is None:
                out[:, cols] = value
            else:
                value = value.astype(bf16)
                mine[:, cols] = value[:HALF]
                other[:, cols] = value[HALF:]

    shapes = [half(4, ROWS, BLOCK)]
    if before is None:
        shapes += [full(ROWS, D)]
    else:
        shapes += [half(HALF, D)] * 2
    operands = (*active, weights, *after) + (() if before is None else (before,))
    return call(kernel, operands, shapes, "decode", MATMUL // 2, mib=20)


def add_core(own, other):
    def kernel(a, b, *refs):
        outs, held = refs[:CHIPS], refs[CHIPS]
        for k in range(CHIPS):
            rows = slice(k * PIECE, (k + 1) * PIECE)
            held[k] = a[rows].astype(f32) + b[rows].astype(f32)
        for k in range(CHIPS):
            outs[k][...] = held[chip_of(k)].astype(bf16)

    return call(
        kernel,
        (own, other),
        [half(PIECE, D)] * CHIPS,
        "add_core",
        1 << 20,
        [pltpu.VMEM((CHIPS, PIECE, D), f32)],
    )


def add_x(terms):
    def kernel(a, b, c, d, out):
        value = a[...].astype(f32) + b[...].astype(f32)
        out[...] = (value + (c[...].astype(f32) + d[...].astype(f32))).astype(bf16)

    return call(kernel, terms, half(PIECE, D), "add_x", 1 << 20)


def error(terms, bias, acts):
    def kernel(*refs):
        t, (b, x, out) = refs[:5], refs[5:]
        value = t[0][...].astype(f32)
        for y in t[1:]:
            value = value + y[...].astype(f32)
        out[...] = ((value + b[...] - x[...].astype(f32)) * (2.0 / ROWS)).astype(bf16)

    return call(kernel, (*terms, bias, acts), half(PIECE, D), "error", 1 << 20)


def join(parts):
    def kernel(*refs):
        out, held = refs[CHIPS:]
        for k in range(CHIPS):
            held[chip_of(k)] = refs[k][...].astype(f32)
        out[...] = jnp.concatenate([held[k] for k in range(CHIPS)], axis=0).astype(bf16)

    return call(
        kernel,
        parts,
        half(HALF, D),
        "join",
        1 << 20,
        [pltpu.VMEM((CHIPS, PIECE, D), f32)],
    )


def backward_far(near_rows, far_rows, rows, norms, weights):
    def kernel(a, b, x, n, w, *refs):
        outs, both = refs[:4], refs[4]
        both[:HALF] = a[...]
        both[HALF:ROWS] = b[...]
        for k, r in enumerate(FAR):
            outs[k][:ROWS] = product(both[:ROWS], w[block_rows(r)])
            outs[k][ROWS:] = split(n[r])
        both[ROWS:] = x[...]

    return call(
        kernel,
        (near_rows, far_rows, rows, norms, weights),
        [half(ROWS + EXTRA, BLOCK)] * 4 + [half(2 * ROWS, D)],
        "backward_far",
        MATMUL // 2,
        mib=8,
    )


def backward_near(both, norms, weights):
    def kernel(e, n, w, *outs):
        for k, r in enumerate(NEAR):
            outs[k][:ROWS] = product(e[:ROWS], w[block_rows(r)])
            outs[k][ROWS:] = split(n[r])

    return call(
        kernel,
        (both, norms, weights),
        [half(ROWS + EXTRA, BLOCK)] * 4,
        "backward_near",
        MATMUL // 2,
        mib=8,
    )


def latent_grad(terms, active):
    def kernel(*refs):
        t, (a, out) = refs[:5], refs[5:]
        total = add_extra(t)
        value = add(t) + SCALE * total[:1]
        out[:ROWS] = (value * (2.0 * a[...].astype(f32))).astype(bf16)
        out[ROWS:] = split(total)

    return call(kernel, (*terms, active), half(ROWS + EXTRA, BLOCK), "latent_grad", 1 << 20)


def gradient(lats, dpres, both, norms, weights, blocks, before=()):
    width = 768
    steps = D // width
    count = len(blocks)

    def kernel(*refs):
        early, late, d = refs[0], refs[1], refs[2 : 2 + count]
        e, n, w = refs[2 + count : 5 + count]
        out, bias, totals, *rest = refs[5 + count + len(before) :]
        lhs, buf, sem = rest[-3:]
        if before:
            bias[...] = refs[6 + count][...]
            totals[...] = refs[7 + count][...]
        else:
            rest[0][...] = jnp.sum(e[:ROWS].astype(f32), axis=0, keepdims=True)
        copies = []
        for k, r in enumerate(blocks):
            l = early[r] if r < 4 else late[r - 4]
            x = d[k][:ROWS]
            lhs[:ROWS] = l
            lhs[ROWS:] = x
            usage = jnp.sum(l.astype(f32), axis=0, keepdims=True)
            column = (SCALE * jnp.broadcast_to(usage, (8, BLOCK)) / n[r]).T[:, :1]
            bias[block_of(r)] = jnp.sum(x.astype(f32), axis=0, keepdims=True)
            totals[block_of(r)] = split_sum(d[k][ROWS:])[:1]
            for i in range(steps):
                cols = slice(i * width, (i + 1) * width)
                g = lax.dot_general(lhs[...], e[:, cols], TN, preferred_element_type=f32)
                g = g + column * w[block_rows(r), cols].astype(f32)
                buf[k, :, cols] = g.astype(bf16)
                copy = pltpu.make_async_copy(
                    buf.at[k, :, cols], out.at[block_rows(r), cols], sem.at[k, i]
                )
                copy.start()
                copies.append(copy)
        for copy in copies:
            copy.wait()

    shapes = [half(F, D), full(LAYERS, 1, BLOCK), full(LAYERS, 1, BLOCK)]
    if not before:
        shapes.append(full(1, D))
    return call(
        kernel,
        (*lats, *[dpres[r] for r in blocks], both, norms, weights, *before),
        shapes,
        "gradient",
        2 * MATMUL * count // LAYERS,
        [
            pltpu.VMEM((2 * ROWS, BLOCK), bf16),
            pltpu.VMEM((count, BLOCK, D), bf16),
            pltpu.SemaphoreType.DMA((count, steps)),
        ],
        12,
        [VMEM] * (5 + count) + ([HBM, VMEM, VMEM] if before else []),
        [HBM] + [VMEM] * (len(shapes) - 1),
        {5 + count: 0} if before else None,
    )


def scatter(terms, ring, pair, add):
    far = [ring(terms[4 + d], d) for d in STEPS]
    near = [ring(terms[d], d) for d in STEPS]
    other = pair(add([terms[4]] + far))
    return [terms[0]] + near + [other]


def gather(own, ring, pair):
    blocks = {0: own, 4: pair(own)}
    for r in (0, 4):
        for d in STEPS:
            blocks[r + d] = ring(blocks[r], 4 - d)
    return blocks


def body(acts, decoder, enc_bias, dec_bias):
    inputs, weights = acts[0], decoder[0]
    bias = enc_bias.reshape(LAYERS, 1, BLOCK)

    *far, rows = encode_far(inputs, weights)
    terms = list(encode_near(rows, weights)) + far
    norms, piece = prepare(rows, weights)
    mine = activate(scatter(terms, move_z, move_y, add_z), bias)
    active = gather(mine, move_z, move_y)
    lat_near, before = decode([active[r] for r in NEAR], weights, NEAR, after=(piece,))
    lat_far, here, there = decode([active[r] for r in FAR], weights, FAR, before)

    pieces = add_core(here, move_core(there))
    own = error(scatter(pieces, move_x, move_lo, add_x), dec_bias, piece)
    got = gather(own, move_x, move_lo)
    here = join([got[r] for r in range(CHIPS)])

    *far, both = backward_far(here, move_core(here), rows, norms, weights)
    terms = list(backward_near(both, norms, weights)) + far
    dpre = latent_grad(scatter(terms, move_z, move_y, add_z), mine)
    dpres = gather(dpre, move_z, move_y)
    out = ()
    for blocks in GROUPS:
        got = gradient((lat_near, lat_far), dpres, both, norms, weights, blocks, out)
        if not out:
            dec_grad = got[3]
        out = tuple(got[:3])
    grad, enc_grad, total = out
    return grad[None], enc_grad.reshape(F), dec_grad, total.reshape(F)


def solution(mesh):
    placed = (P("layer", None, None), P("layer", "latent", None), P("latent"), P("layer", None))
    return jax.shard_map(
        body,
        mesh=mesh,
        in_specs=placed,
        out_specs=(P("layer", "latent", None), P("latent"), P("layer", None), P("latent")),
        check_vma=False,
    )
```

```python
import jax
import jax.numpy as jnp
from jax import lax
from jax.experimental import pallas as pl
from jax.experimental.pallas import tpu as pltpu
from jax.sharding import PartitionSpec as P

penalty_weight = 3.0
norm_eps = 1e-06

D = 2304
ROWS = 384
HALF = ROWS // 2
F = 2048
LAYERS = 8
BLOCK = F // LAYERS
CHIPS = 8
PIECE = HALF // CHIPS
EXTRA = 16
GROUPS = ((0,), (4, 2, 1, 3), (5, 7, 6))
READY = (4, 5, 6, 7)
SCALE = penalty_weight / ROWS
MATMUL = 2 * ROWS * F * D

NEAR = (0, 1, 2, 3)
FAR = (4, 5, 6, 7)
SIDES = (1, 3)

f32 = jnp.float32
bf16 = jnp.bfloat16
NT = (((1,), (1,)), ((), ()))
TN = (((0,), (0,)), ((), ()))
VMEM = pl.BlockSpec(memory_space=pltpu.VMEM)
HBM = pl.BlockSpec(memory_space=pl.ANY)


def half(*shape):
    return jax.ShapeDtypeStruct(shape, bf16)


def full(*shape):
    return jax.ShapeDtypeStruct(shape, f32)


def call(kernel, operands, out_shape, name, flops, scratch=(), mib=4, places=None, outs=None, aliases=None):
    many = isinstance(out_shape, (list, tuple))
    return pl.pallas_call(
        kernel,
        in_specs=places or [VMEM] * len(operands),
        out_specs=outs or ([VMEM] * len(out_shape) if many else VMEM),
        out_shape=out_shape,
        scratch_shapes=list(scratch),
        input_output_aliases=aliases or {},
        compiler_params=pltpu.CompilerParams(vmem_limit_bytes=mib << 20),
        cost_estimate=pl.CostEstimate(flops=flops, bytes_accessed=flops // 400, transcendentals=0),
        name=name,
    )(*operands)


def move_y(x):
    return lax.ppermute(x, "layer", [(i, i ^ 4) for i in range(8)])


def move_z(x, r):
    return lax.ppermute(x, "layer", [(i, i ^ r) for i in range(8)])


def move_core(x):
    return lax.ppermute(x, "latent", [(i, i ^ 1) for i in range(16)])


def move_lo(x):
    return lax.ppermute(x, "latent", [(i, i ^ 8) for i in range(16)])


def move_x(x, r):
    return lax.ppermute(x, "latent", [(i, i ^ (2 * r)) for i in range(16)])


def block_of(r):
    return lax.axis_index("layer") ^ r


def chip_of(r):
    return (lax.axis_index("latent") >> 1) ^ r


def block_rows(r):
    return pl.ds(pl.multiple_of(block_of(r) * BLOCK, BLOCK), BLOCK)


def split_sum(rows):
    return rows[:8].astype(f32) + rows[8:].astype(f32)


def split(value):
    high = value.astype(bf16)
    low = (value - high.astype(f32)).astype(bf16)
    return jnp.concatenate([high, low], axis=0)


def product(rows, weights):
    return lax.dot_general(rows, weights, NT, preferred_element_type=f32).astype(bf16)


def encode_far(acts, weights):
    def kernel(a, w, *refs):
        rows = refs[4]
        c = lax.axis_index("latent") & 1
        for k, source in enumerate((c, 1 - c)):
            rows[k * HALF : (k + 1) * HALF] = a[pl.ds(pl.multiple_of(source * HALF, HALF), HALF)]
        for k, r in enumerate(FAR):
            refs[k][...] = product(rows[...], w[block_rows(r)])

    return call(
        kernel,
        (acts, weights),
        [half(ROWS, BLOCK)] * 4 + [half(ROWS, D)],
        "encode_far",
        MATMUL // 2,
        mib=8,
    )


def encode_near(rows, weights):
    def kernel(a, w, *outs):
        for k, r in enumerate(NEAR):
            outs[k][...] = product(a[...], w[block_rows(r)])

    return call(
        kernel, (rows, weights), [half(ROWS, BLOCK)] * 4, "encode_near", MATMUL // 2, mib=8
    )


def prepare(rows, weights):
    def kernel(a, w, norms, piece, held):
        for r in range(LAYERS):
            wb = w[block_rows(r)]
            squares = jnp.zeros((BLOCK, 128), f32)
            for i in range(D // 128):
                x = wb[:, i * 128 : (i + 1) * 128].astype(f32)
                squares = squares + x * x
            total = lax.dot_general(
                jnp.ones((8, 128), f32),
                squares,
                NT,
                precision=lax.Precision.HIGHEST,
                preferred_element_type=f32,
            )
            norms[r] = jnp.sqrt(total + norm_eps)
        value = a[:HALF].astype(f32)
        for k in range(CHIPS):
            held[k] = value[k * PIECE : (k + 1) * PIECE]
        piece[...] = held[chip_of(0)].astype(bf16)

    return call(
        kernel,
        (rows, weights),
        [full(LAYERS, 8, BLOCK), half(PIECE, D)],
        "prepare",
        1 << 30,
        [pltpu.VMEM((CHIPS, PIECE, D), f32)],
        8,
    )


def add(terms):
    value = terms[0][:ROWS].astype(f32)
    for x in terms[1:]:
        value = value + x[:ROWS].astype(f32)
    return value


def add_extra(terms):
    return sum(split_sum(x[ROWS:]) for x in terms)


def add_z(terms):
    extra = terms[0].shape[0] - ROWS

    def kernel(*refs):
        *t, out = refs
        out[:ROWS] = add(t).astype(bf16)
        if extra:
            out[ROWS:] = split(add_extra(t))

    return call(kernel, terms, half(*terms[0].shape), "add_z", 1 << 20)


def activate(terms, bias):
    def kernel(*refs):
        t, (b, out) = refs[:5], refs[5:]
        out[...] = jnp.maximum(add(t) + b[block_of(0)], 0.0).astype(bf16)

    return call(kernel, (*terms, bias), half(ROWS, BLOCK), "activate", 1 << 20)


def decode(active, weights, blocks, before=None, after=()):
    width = 768

    def kernel(*refs):
        g, w, refs = refs[:4], refs[4], refs[5:]
        if before is not None:
            acc, lat, mine, other = refs
        else:
            lat, out = refs[len(after) :]
        for k in range(4):
            x = g[k][...].astype(f32)
            lat[k] = (x * x).astype(bf16)
        for i in range(D // width):
            cols = slice(i * width, (i + 1) * width)
            value = None if before is None else acc[:, cols]
            for k, r in enumerate(blocks):
                term = jnp.dot(lat[k], w[block_rows(r), cols], preferred_element_type=f32)
                value = term if value is None else value + term
            if before is None:
                out[:, cols] = value
            else:
                value = value.astype(bf16)
                mine[:, cols] = value[:HALF]
                other[:, cols] = value[HALF:]

    shapes = [half(4, ROWS, BLOCK)]
    if before is None:
        shapes += [full(ROWS, D)]
    else:
        shapes += [half(HALF, D)] * 2
    operands = (*active, weights, *after) + (() if before is None else (before,))
    return call(kernel, operands, shapes, "decode", MATMUL // 2, mib=20)


def add_core(own, other):
    def kernel(a, b, *refs):
        outs, held = refs[:CHIPS], refs[CHIPS]
        for k in range(CHIPS):
            rows = slice(k * PIECE, (k + 1) * PIECE)
            held[k] = a[rows].astype(f32) + b[rows].astype(f32)
        for k in range(CHIPS):
            outs[k][...] = held[chip_of(k)].astype(bf16)

    return call(
        kernel,
        (own, other),
        [half(PIECE, D)] * CHIPS,
        "add_core",
        1 << 20,
        [pltpu.VMEM((CHIPS, PIECE, D), f32)],
    )


def add_x(terms):
    def kernel(*refs):
        *t, out = refs
        value = t[0][...].astype(f32)
        for x in t[1:]:
            value = value + x[...].astype(f32)
        out[...] = value.astype(bf16)

    return call(kernel, terms, half(PIECE, D), "add_x", 1 << 20)


def error(terms, bias, acts):
    def kernel(*refs):
        t, (b, x, out) = refs[:5], refs[5:]
        value = t[0][...].astype(f32)
        for y in t[1:]:
            value = value + y[...].astype(f32)
        out[...] = ((value + b[...] - x[...].astype(f32)) * (2.0 / ROWS)).astype(bf16)

    return call(kernel, (*terms, bias, acts), half(PIECE, D), "error", 1 << 20)


def join(parts):
    def kernel(*refs):
        out, held = refs[4:]
        for k in range(4):
            held[chip_of(k) & 3] = refs[k][...].astype(f32)
        out[...] = jnp.concatenate([held[k] for k in range(4)], axis=0).astype(bf16)

    return call(
        kernel,
        parts,
        half(4 * PIECE, D),
        "join",
        1 << 20,
        [pltpu.VMEM((4, PIECE, D), f32)],
    )


def backward_far(parts, rows, norms, weights):
    def kernel(*refs):
        p, (x, n, w), outs, both = refs[:4], refs[4:7], refs[7:11], refs[11]
        low = lax.axis_index("latent") >> 3
        for k in range(4):
            at = (k // 2) * HALF + (low ^ (k % 2)) * (HALF // 2)
            both[pl.ds(pl.multiple_of(at, HALF // 2), HALF // 2)] = p[k][...]
        for k, r in enumerate(FAR):
            outs[k][:ROWS] = product(both[:ROWS], w[block_rows(r)])
            outs[k][ROWS:] = split(n[r])
        both[ROWS:] = x[...]

    return call(
        kernel,
        (*parts, rows, norms, weights),
        [half(ROWS + EXTRA, BLOCK)] * 4 + [half(2 * ROWS, D)],
        "backward_far",
        MATMUL // 2,
        mib=8,
    )


def backward_near(both, norms, weights):
    def kernel(e, n, w, *outs):
        for k, r in enumerate(NEAR):
            outs[k][:ROWS] = product(e[:ROWS], w[block_rows(r)])
            outs[k][ROWS:] = split(n[r])

    return call(
        kernel,
        (both, norms, weights),
        [half(ROWS + EXTRA, BLOCK)] * 4,
        "backward_near",
        MATMUL // 2,
        mib=8,
    )


def latent_grad(terms, active, ready):
    def kernel(*refs):
        t, (a, _, out) = refs[:5], refs[5:]
        total = add_extra(t)
        value = add(t) + SCALE * total[:1]
        out[:ROWS] = (value * (2.0 * a[...].astype(f32))).astype(bf16)
        out[ROWS:] = split(total)

    return call(
        kernel,
        (*terms, active, ready),
        half(ROWS + EXTRA, BLOCK),
        "latent_grad",
        1 << 20,
        places=[VMEM] * 6 + [HBM],
    )


def prepare_gradient(lats, both, norms, weights):
    width = 768

    def kernel(early, late, e, n, w, out):
        for k, r in enumerate(READY):
            l = early[r] if r < 4 else late[r - 4]
            column = penalty(l, n[r])
            for i in range(D // width):
                cols = slice(i * width, (i + 1) * width)
                g = lax.dot_general(l, e[:ROWS, cols], TN, preferred_element_type=f32)
                out[k, :, cols] = (g + column * w[block_rows(r), cols].astype(f32)).astype(bf16)

    return call(
        kernel,
        (*lats, both, norms, weights),
        half(len(READY), BLOCK, D),
        "prepare_gradient",
        MATMUL * len(READY) // LAYERS,
        mib=8,
    )


def penalty(lat, norms):
    usage = jnp.sum(lat.astype(f32), axis=0, keepdims=True)
    return (SCALE * jnp.broadcast_to(usage, (8, BLOCK)) / norms).T[:, :1]


def gradient(lats, dpres, both, norms, weights, ready, blocks, before=None, last=False):
    width = 768
    steps = D // width
    count = len(blocks)
    used = tuple(range(LAYERS)) if last else blocks
    first = before is None

    def kernel(early, late, *refs):
        d = dict(zip(used, refs))
        e, n, w, p = refs[len(used) : len(used) + 4]
        refs = refs[len(used) + 4 + (not first) :]
        out, lhs, buf, sem = refs[0], *refs[-3:]
        copies = []
        if first:
            bias, held, bias_sem = refs[1:4]
            held[...] = jnp.sum(e[:ROWS].astype(f32), axis=0, keepdims=True)
            copies.append(pltpu.make_async_copy(held, bias, bias_sem.at[0]))
        if last:
            enc, totals, held, sums, bias_sem = refs[1:6]
            for r in range(LAYERS):
                x = d[r][:ROWS].astype(f32)
                held[block_of(r)] = jnp.sum(x, axis=0, keepdims=True)
                sums[block_of(r)] = split_sum(d[r][ROWS:])[:1]
            copies.append(pltpu.make_async_copy(held, enc, bias_sem.at[0]))
            copies.append(pltpu.make_async_copy(sums, totals, bias_sem.at[1]))
        for copy in copies:
            copy.start()
        for k, r in enumerate(blocks):
            if r not in READY:
                l = early[r] if r < 4 else late[r - 4]
                lhs[:ROWS] = l
                lhs[ROWS:] = d[r][:ROWS]
                column = penalty(l, n[r])
            for i in range(steps):
                cols = slice(i * width, (i + 1) * width)
                if r in READY:
                    x = d[r][:ROWS]
                    g = lax.dot_general(x, e[ROWS:, cols], TN, preferred_element_type=f32)
                    g = g + p[READY.index(r), :, cols].astype(f32)
                else:
                    g = lax.dot_general(lhs[...], e[:, cols], TN, preferred_element_type=f32)
                    g = g + column * w[block_rows(r), cols].astype(f32)
                buf[k, :, cols] = g.astype(bf16)
                copy = pltpu.make_async_copy(
                    buf.at[k, :, cols], out.at[block_rows(r), cols], sem.at[k, i]
                )
                copy.start()
                copies.append(copy)
        for copy in copies:
            copy.wait()

    shapes, scratch = [half(F, D)], []
    if first:
        shapes.append(full(1, D))
        scratch += [pltpu.VMEM((1, D), f32), pltpu.SemaphoreType.DMA((1,))]
    if last:
        shapes += [full(LAYERS, 1, BLOCK)] * 2
        scratch += [pltpu.VMEM((LAYERS, 1, BLOCK), f32)] * 2 + [pltpu.SemaphoreType.DMA((2,))]
    operands = (*lats, *[dpres[r] for r in used], both, norms, weights, ready)
    return call(
        kernel,
        operands if first else (*operands, before),
        shapes,
        "gradient",
        2 * MATMUL * count // LAYERS,
        scratch
        + [
            pltpu.VMEM((2 * ROWS, BLOCK), bf16),
            pltpu.VMEM((count, BLOCK, D), bf16),
            pltpu.SemaphoreType.DMA((count, steps)),
        ],
        12,
        [VMEM] * len(operands) + ([] if first else [HBM]),
        [HBM] * len(shapes),
        None if first else {len(operands): 0},
    )


def scatter(terms, ring, pair, add):
    cross = pair(terms[6])
    far = [ring(terms[4 + d], d) for d in SIDES]
    near = [ring(terms[d], d) for d in SIDES]
    other = pair(add([terms[4]] + far))
    return [terms[0]] + near + [ring(add([terms[2], cross]), 2), other]


def gather(own, ring, pair):
    blocks = {0: own, 4: pair(own), 2: ring(own, 2)}
    for r in (0, 4):
        for d in SIDES:
            blocks[r + d] = ring(blocks[r], d)
    blocks[6] = pair(blocks[2])
    return blocks


def body(acts, decoder, enc_bias, dec_bias):
    inputs, weights = acts[0], decoder[0]
    bias = enc_bias.reshape(LAYERS, 1, BLOCK)

    *far, rows = encode_far(inputs, weights)
    terms = list(encode_near(rows, weights)) + far
    norms, piece = prepare(rows, weights)
    mine = activate(scatter(terms, move_z, move_y, add_z), bias)
    active = gather(mine, move_z, move_y)
    lat_near, before = decode([active[r] for r in NEAR], weights, NEAR)
    lat_far, here, there = decode([active[r] for r in FAR], weights, FAR, before)

    pieces = add_core(here, move_core(there))
    own = error(scatter(pieces, move_x, move_lo, add_x), dec_bias, piece)
    got = gather(own, move_x, move_lo)
    here = [join([got[r] for r in blocks]) for blocks in (NEAR, FAR)]
    errors = here + [move_core(x) for x in here]

    *far, both = backward_far(errors, rows, norms, weights)
    terms = list(backward_near(both, norms, weights)) + far
    ready = prepare_gradient((lat_near, lat_far), both, norms, weights)
    dpre = latent_grad(scatter(terms, move_z, move_y, add_z), mine, ready)
    dpres = gather(dpre, move_z, move_y)
    grad = None
    for i, blocks in enumerate(GROUPS):
        last = i == len(GROUPS) - 1
        out = gradient((lat_near, lat_far), dpres, both, norms, weights, ready, blocks, grad, last)
        grad = out[0]
        if i == 0:
            dec_grad = out[1]
    enc_grad, total = out[1:]
    return grad[None], enc_grad.reshape(F), dec_grad, total.reshape(F)


def solution(mesh):
    placed = (P("layer", None, None), P("layer", "latent", None), P("latent"), P("layer", None))
    return jax.shard_map(
        body,
        mesh=mesh,
        in_specs=placed,
        out_specs=(P("layer", "latent", None), P("latent"), P("layer", None), P("latent")),
        check_vma=False,
    )
```

```python
import jax
import jax.numpy as jnp
from jax import lax
from jax.experimental import pallas as pl
from jax.experimental.pallas import tpu as pltpu
from jax.sharding import PartitionSpec as P

penalty_weight = 3.0
norm_eps = 1e-06

D = 2304
ROWS = 384
HALF = ROWS // 2
F = 2048
LAYERS = 8
BLOCK = F // LAYERS
CHIPS = 8
QUARTER = HALF // 2
PIECE = HALF // CHIPS
EXTRA = 16
GROUPS = ((0,), (4, 2, 1, 3), (5, 7, 6))
READY = (1, 2, 3, 4, 5, 6, 7)
SENT = ((5, 7, 6), (1, 3), (4, 0, 2))
BACK = ((0, 1, 2, 3), (4, 5, 7), (6,))
SCALE = penalty_weight / ROWS
MATMUL = 2 * ROWS * F * D

SIDES = (1, 3)

f32 = jnp.float32
bf16 = jnp.bfloat16
NT = (((1,), (1,)), ((), ()))
TN = (((0,), (0,)), ((), ()))
VMEM = pl.BlockSpec(memory_space=pltpu.VMEM)
HBM = pl.BlockSpec(memory_space=pl.ANY)


def half(*shape):
    return jax.ShapeDtypeStruct(shape, bf16)


def full(*shape):
    return jax.ShapeDtypeStruct(shape, f32)


def call(kernel, operands, out_shape, name, flops, scratch=(), mib=4, places=None, outs=None, aliases=None):
    many = isinstance(out_shape, (list, tuple))
    return pl.pallas_call(
        kernel,
        in_specs=places or [VMEM] * len(operands),
        out_specs=outs or ([VMEM] * len(out_shape) if many else VMEM),
        out_shape=out_shape,
        scratch_shapes=list(scratch),
        input_output_aliases=aliases or {},
        compiler_params=pltpu.CompilerParams(vmem_limit_bytes=mib << 20),
        cost_estimate=pl.CostEstimate(flops=flops, bytes_accessed=flops // 400, transcendentals=0),
        name=name,
    )(*operands)


def move_y(x):
    return lax.ppermute(x, "layer", [(i, i ^ 4) for i in range(8)])


def move_z(x, r):
    return lax.ppermute(x, "layer", [(i, i ^ r) for i in range(8)])


def move_core(x):
    return lax.ppermute(x, "latent", [(i, i ^ 1) for i in range(16)])


def move_lo(x):
    return lax.ppermute(x, "latent", [(i, i ^ 8) for i in range(16)])


def move_x(x, r):
    return lax.ppermute(x, "latent", [(i, i ^ (2 * r)) for i in range(16)])


def block_of(r):
    return lax.axis_index("layer") ^ r


def chip_of(r):
    return (lax.axis_index("latent") >> 1) ^ r


def block_rows(r):
    return pl.ds(pl.multiple_of(block_of(r) * BLOCK, BLOCK), BLOCK)


def split_sum(rows):
    return rows[:8].astype(f32) + rows[8:].astype(f32)


def split(value):
    high = value.astype(bf16)
    low = (value - high.astype(f32)).astype(bf16)
    return jnp.concatenate([high, low], axis=0)


def product(rows, weights):
    return lax.dot_general(rows, weights, NT, preferred_element_type=f32).astype(bf16)


def encode_first(acts, weights, blocks):
    def kernel(a, w, *refs):
        rows = refs[-1]
        latent = lax.axis_index("latent")
        for k in range(4):
            at = ((latent & 1) ^ (k // 2)) * HALF + ((latent >> 3) ^ (k % 2)) * QUARTER
            rows[k * QUARTER : (k + 1) * QUARTER] = a[pl.ds(pl.multiple_of(at, QUARTER), QUARTER)]
        for k, r in enumerate(blocks):
            refs[k][...] = product(rows[...], w[block_rows(r)])

    return call(
        kernel,
        (acts, weights),
        [half(ROWS, BLOCK)] * len(blocks) + [half(ROWS, D)],
        "encode_first",
        MATMUL * len(blocks) // LAYERS,
        mib=8,
    )


def encode(rows, weights, blocks):
    def kernel(a, w, *outs):
        for out, r in zip(outs, blocks):
            out[...] = product(a[...], w[block_rows(r)])

    return call(
        kernel,
        (rows, weights),
        [half(ROWS, BLOCK)] * len(blocks),
        "encode",
        MATMUL * len(blocks) // LAYERS,
        mib=8,
    )


def prepare(rows, weights):
    def kernel(a, w, norms, piece, held):
        for r in range(LAYERS):
            wb = w[block_rows(r)]
            squares = jnp.zeros((BLOCK, 128), f32)
            for i in range(D // 128):
                x = wb[:, i * 128 : (i + 1) * 128].astype(f32)
                squares = squares + x * x
            total = lax.dot_general(
                jnp.ones((8, 128), f32),
                squares,
                NT,
                precision=lax.Precision.HIGHEST,
                preferred_element_type=f32,
            )
            norms[r] = jnp.sqrt(total + norm_eps)
        value = a[:QUARTER].astype(f32)
        for k in range(4):
            held[k] = value[k * PIECE : (k + 1) * PIECE]
        piece[...] = held[chip_of(0) & 3].astype(bf16)

    return call(
        kernel,
        (rows, weights),
        [full(LAYERS, 8, BLOCK), half(PIECE, D)],
        "prepare",
        1 << 30,
        [pltpu.VMEM((4, PIECE, D), f32)],
        8,
    )


def add(terms):
    value = terms[0][:ROWS].astype(f32)
    for x in terms[1:]:
        value = value + x[:ROWS].astype(f32)
    return value


def add_extra(terms):
    return sum(split_sum(x[ROWS:]) for x in terms)


def add_z(terms):
    extra = terms[0].shape[0] - ROWS

    def kernel(*refs):
        *t, out = refs
        out[:ROWS] = add(t).astype(bf16)
        if extra:
            out[ROWS:] = split(add_extra(t))

    return call(kernel, terms, half(*terms[0].shape), "add_z", 1 << 20)


def activate(terms, bias):
    def kernel(*refs):
        t, (b, out) = refs[:5], refs[5:]
        out[...] = jnp.maximum(add(t) + b[block_of(0)], 0.0).astype(bf16)

    return call(kernel, (*terms, bias), half(ROWS, BLOCK), "activate", 1 << 20)


def decode(active, weights, blocks, before, last):
    width = 768
    count = len(blocks)

    def kernel(*refs):
        g, w = refs[:count], refs[count]
        lat, *outs = refs[count + 1 + len(before) :]
        for k in range(count):
            x = g[k][...].astype(f32)
            lat[k] = (x * x).astype(bf16)
        for i in range(D // width):
            cols = slice(i * width, (i + 1) * width)
            value = refs[count + 1][:, cols] if before else None
            for k, r in enumerate(blocks):
                term = jnp.dot(lat[k], w[block_rows(r), cols], preferred_element_type=f32)
                value = term if value is None else value + term
            if last:
                for k in range(4):
                    outs[k][:, cols] = value[k * QUARTER : (k + 1) * QUARTER].astype(bf16)
            else:
                outs[0][:, cols] = value

    return call(
        kernel,
        (*active, weights, *before),
        [half(count, ROWS, BLOCK)] + ([half(QUARTER, D)] * 4 if last else [full(ROWS, D)]),
        "decode",
        MATMUL * count // LAYERS,
        mib=12,
    )


def latents_of(lats, r):
    for lat, blocks in zip(lats, BACK):
        if r in blocks:
            return lat[blocks.index(r)]


def add_core(own, other):
    def kernel(a, b, *refs):
        outs, held = refs[:4], refs[4]
        total = a[...].astype(f32) + b[...].astype(f32)
        for k in range(4):
            held[k] = total[k * PIECE : (k + 1) * PIECE]
        for k in range(4):
            outs[k][...] = held[chip_of(k) & 3].astype(bf16)

    return call(
        kernel,
        (own, other),
        [half(PIECE, D)] * 4,
        "add_core",
        1 << 20,
        [pltpu.VMEM((4, PIECE, D), f32)],
    )


def add_x(terms):
    def kernel(*refs):
        *t, out = refs
        value = t[0][...].astype(f32)
        for x in t[1:]:
            value = value + x[...].astype(f32)
        out[...] = value.astype(bf16)

    return call(kernel, terms, half(PIECE, D), "add_x", 1 << 20)


def error(terms, bias, acts):
    def kernel(*refs):
        t, (b, x, out) = refs[:5], refs[5:]
        value = t[0][...].astype(f32)
        for y in t[1:]:
            value = value + y[...].astype(f32)
        out[...] = ((value + b[...] - x[...].astype(f32)) * (2.0 / ROWS)).astype(bf16)

    return call(kernel, (*terms, bias, acts), half(PIECE, D), "error", 1 << 20)


def join(parts):
    def kernel(*refs):
        out, held = refs[4:]
        for k in range(4):
            held[chip_of(k) & 3] = refs[k][...].astype(f32)
        out[...] = jnp.concatenate([held[k] for k in range(4)], axis=0).astype(bf16)

    return call(
        kernel,
        parts,
        half(4 * PIECE, D),
        "join",
        1 << 20,
        [pltpu.VMEM((4, PIECE, D), f32)],
    )


def backward_first(parts, rows, norms, weights, blocks):
    count = len(blocks)

    def kernel(*refs):
        p, (x, n, w), outs, both = refs[:4], refs[4:7], refs[7 : 7 + count], refs[7 + count]
        for k in range(4):
            both[k * QUARTER : (k + 1) * QUARTER] = p[k][...]
        for out, r in zip(outs, blocks):
            out[:ROWS] = product(both[:ROWS], w[block_rows(r)])
            out[ROWS:] = split(n[r])
        both[ROWS:] = x[...]

    return call(
        kernel,
        (*parts, rows, norms, weights),
        [half(ROWS + EXTRA, BLOCK)] * count + [half(2 * ROWS, D)],
        "backward_first",
        MATMUL * count // LAYERS,
        mib=8,
    )


def backward(both, norms, weights, blocks):
    def kernel(e, n, w, *outs):
        for out, r in zip(outs, blocks):
            out[:ROWS] = product(e[:ROWS], w[block_rows(r)])
            out[ROWS:] = split(n[r])

    return call(
        kernel,
        (both, norms, weights),
        [half(ROWS + EXTRA, BLOCK)] * len(blocks),
        "backward",
        MATMUL * len(blocks) // LAYERS,
        mib=8,
    )


def latent_grad(terms, active, ready):
    def kernel(*refs):
        t, (a, _, out) = refs[:5], refs[5:]
        total = add_extra(t)
        value = add(t) + SCALE * total[:1]
        out[:ROWS] = (value * (2.0 * a[...].astype(f32))).astype(bf16)
        out[ROWS:] = split(total)

    return call(
        kernel,
        (*terms, active, ready),
        half(ROWS + EXTRA, BLOCK),
        "latent_grad",
        1 << 20,
        places=[VMEM] * 6 + [HBM],
    )


def prepare_gradient(lats, both, norms, weights):
    width = 768

    def kernel(*refs):
        ls, (e, n, w, out) = refs[: len(BACK)], refs[len(BACK) :]
        for k, r in enumerate(READY):
            l = latents_of(ls, r)
            column = penalty(l, n[r])
            for i in range(D // width):
                cols = slice(i * width, (i + 1) * width)
                g = lax.dot_general(l, e[:ROWS, cols], TN, preferred_element_type=f32)
                out[k, :, cols] = (g + column * w[block_rows(r), cols].astype(f32)).astype(bf16)

    return call(
        kernel,
        (*lats, both, norms, weights),
        half(len(READY), BLOCK, D),
        "prepare_gradient",
        MATMUL * len(READY) // LAYERS,
        mib=8,
    )


def penalty(lat, norms):
    usage = jnp.sum(lat.astype(f32), axis=0, keepdims=True)
    return (SCALE * jnp.broadcast_to(usage, (8, BLOCK)) / norms).T[:, :1]


def gradient(lats, dpres, both, norms, weights, ready, blocks, before=None, last=False):
    width = 768
    steps = D // width
    count = len(blocks)
    used = tuple(range(LAYERS)) if last else blocks
    first = before is None

    def kernel(*refs):
        ls, refs = refs[: len(BACK)], refs[len(BACK) :]
        d = dict(zip(used, refs))
        e, n, w, p = refs[len(used) : len(used) + 4]
        refs = refs[len(used) + 4 + (not first) :]
        out, lhs, buf, sem = refs[0], *refs[-3:]
        copies = []
        if first:
            bias, held, bias_sem = refs[1:4]
            held[...] = jnp.sum(e[:ROWS].astype(f32), axis=0, keepdims=True)
            copies.append(pltpu.make_async_copy(held, bias, bias_sem.at[0]))
        if last:
            enc, totals, held, sums, bias_sem = refs[1:6]
            for r in range(LAYERS):
                x = d[r][:ROWS].astype(f32)
                held[block_of(r)] = jnp.sum(x, axis=0, keepdims=True)
                sums[block_of(r)] = split_sum(d[r][ROWS:])[:1]
            copies.append(pltpu.make_async_copy(held, enc, bias_sem.at[0]))
            copies.append(pltpu.make_async_copy(sums, totals, bias_sem.at[1]))
        for copy in copies:
            copy.start()
        for k, r in enumerate(blocks):
            if r not in READY:
                l = latents_of(ls, r)
                lhs[:ROWS] = l
                lhs[ROWS:] = d[r][:ROWS]
                column = penalty(l, n[r])
            for i in range(steps):
                cols = slice(i * width, (i + 1) * width)
                if r in READY:
                    x = d[r][:ROWS]
                    g = lax.dot_general(x, e[ROWS:, cols], TN, preferred_element_type=f32)
                    g = g + p[READY.index(r), :, cols].astype(f32)
                else:
                    g = lax.dot_general(lhs[...], e[:, cols], TN, preferred_element_type=f32)
                    g = g + column * w[block_rows(r), cols].astype(f32)
                buf[k, :, cols] = g.astype(bf16)
                copy = pltpu.make_async_copy(
                    buf.at[k, :, cols], out.at[block_rows(r), cols], sem.at[k, i]
                )
                copy.start()
                copies.append(copy)
        for copy in copies:
            copy.wait()

    shapes, scratch = [half(F, D)], []
    if first:
        shapes.append(full(1, D))
        scratch += [pltpu.VMEM((1, D), f32), pltpu.SemaphoreType.DMA((1,))]
    if last:
        shapes += [full(LAYERS, 1, BLOCK)] * 2
        scratch += [pltpu.VMEM((LAYERS, 1, BLOCK), f32)] * 2 + [pltpu.SemaphoreType.DMA((2,))]
    operands = (*lats, *[dpres[r] for r in used], both, norms, weights, ready)
    return call(
        kernel,
        operands if first else (*operands, before),
        shapes,
        "gradient",
        2 * MATMUL * count // LAYERS,
        scratch
        + [
            pltpu.VMEM((2 * ROWS, BLOCK), bf16),
            pltpu.VMEM((count, BLOCK, D), bf16),
            pltpu.SemaphoreType.DMA((count, steps)),
        ],
        12,
        [VMEM] * len(operands) + ([] if first else [HBM]),
        [HBM] * len(shapes),
        None if first else {len(operands): 0},
    )


def scatter(terms, ring, pair, add):
    cross = pair(terms[6])
    far = [ring(terms[4 + d], d) for d in SIDES]
    near = [ring(terms[d], d) for d in SIDES]
    other = pair(add([terms[4]] + far))
    return [terms[0]] + near + [ring(add([terms[2], cross]), 2), other]


def gather(own, ring, pair):
    blocks = {0: own, 4: pair(own), 2: ring(own, 2)}
    for r in (0, 4):
        for d in SIDES:
            blocks[r + d] = ring(blocks[r], d)
    blocks[6] = pair(blocks[2])
    return blocks


def body(acts, decoder, enc_bias, dec_bias):
    inputs, weights = acts[0], decoder[0]
    bias = enc_bias.reshape(LAYERS, 1, BLOCK)

    *out, rows = encode_first(inputs, weights, SENT[0])
    for blocks in SENT[1:]:
        out += encode(rows, weights, blocks)
    terms = dict(zip(sum(SENT, ()), out))
    norms, piece = prepare(rows, weights)
    mine = activate(scatter(terms, move_z, move_y, add_z), bias)
    active = gather(mine, move_z, move_y)
    lats, before = [], ()
    for blocks in BACK:
        last = blocks is BACK[-1]
        lat, *before = decode([active[r] for r in blocks], weights, blocks, before, last)
        lats.append(lat)

    far, near = [add_core(before[k], move_core(before[2 + k])) for k in (1, 0)]
    own = error(scatter([*near, *far], move_x, move_lo, add_x), dec_bias, piece)
    got = gather(own, move_x, move_lo)
    errors = [join([got[r + k] for k in range(4)]) for r in (0, 4)]
    errors += [move_core(x) for x in errors]

    *out, both = backward_first(errors, rows, norms, weights, SENT[0])
    for blocks in SENT[1:]:
        out += backward(both, norms, weights, blocks)
    terms = dict(zip(sum(SENT, ()), out))
    ready = prepare_gradient(lats, both, norms, weights)
    dpre = latent_grad(scatter(terms, move_z, move_y, add_z), mine, ready)
    dpres = gather(dpre, move_z, move_y)
    grad = None
    for i, blocks in enumerate(GROUPS):
        last = i == len(GROUPS) - 1
        out = gradient(lats, dpres, both, norms, weights, ready, blocks, grad, last)
        grad = out[0]
        if i == 0:
            dec_grad = out[1]
    enc_grad, total = out[1:]
    return grad[None], enc_grad.reshape(F), dec_grad, total.reshape(F)


def solution(mesh):
    placed = (P("layer", None, None), P("layer", "latent", None), P("latent"), P("layer", None))
    return jax.shard_map(
        body,
        mesh=mesh,
        in_specs=placed,
        out_specs=(P("layer", "latent", None), P("latent"), P("layer", None), P("latent")),
        check_vma=False,
    )
```

```python
import jax
import jax.numpy as jnp
from jax import lax
from jax.experimental import pallas as pl
from jax.experimental.pallas import tpu as pltpu
from jax.sharding import PartitionSpec as P

penalty_weight = 3.0
norm_eps = 1e-06

D = 2304
ROWS = 384
HALF = ROWS // 2
F = 2048
LAYERS = 8
BLOCK = F // LAYERS
CHIPS = 8
QUARTER = HALF // 2
PIECE = HALF // CHIPS
EXTRA = 16
GROUPS = ((0,), (4, 2, 1, 3), (5, 7, 6))
READY = (1, 2, 3, 4, 5, 6, 7)
SENT = ((5, 7, 6), (1, 3), (4, 0, 2))
BACK = ((0, 1, 2, 3), (4, 5, 7), (6,))
SCALE = penalty_weight / ROWS
MATMUL = 2 * ROWS * F * D

SIDES = (1, 3)

f32 = jnp.float32
bf16 = jnp.bfloat16
NT = (((1,), (1,)), ((), ()))
TN = (((0,), (0,)), ((), ()))
VMEM = pl.BlockSpec(memory_space=pltpu.VMEM)
HBM = pl.BlockSpec(memory_space=pl.ANY)


def half(*shape):
    return jax.ShapeDtypeStruct(shape, bf16)


def full(*shape):
    return jax.ShapeDtypeStruct(shape, f32)


def call(kernel, operands, out_shape, name, flops, scratch=(), mib=4, places=None, outs=None, aliases=None):
    many = isinstance(out_shape, (list, tuple))
    return pl.pallas_call(
        kernel,
        in_specs=places or [VMEM] * len(operands),
        out_specs=outs or ([VMEM] * len(out_shape) if many else VMEM),
        out_shape=out_shape,
        scratch_shapes=list(scratch),
        input_output_aliases=aliases or {},
        compiler_params=pltpu.CompilerParams(vmem_limit_bytes=mib << 20),
        cost_estimate=pl.CostEstimate(flops=flops, bytes_accessed=flops // 400, transcendentals=0),
        name=name,
    )(*operands)


def move_y(x):
    return lax.ppermute(x, "layer", [(i, i ^ 4) for i in range(8)])


def move_z(x, r):
    return lax.ppermute(x, "layer", [(i, i ^ r) for i in range(8)])


def move_core(x):
    return lax.ppermute(x, "latent", [(i, i ^ 1) for i in range(16)])


def move_lo(x):
    return lax.ppermute(x, "latent", [(i, i ^ 8) for i in range(16)])


def move_x(x, r):
    return lax.ppermute(x, "latent", [(i, i ^ (2 * r)) for i in range(16)])


def block_of(r):
    return lax.axis_index("layer") ^ r


def chip_of(r):
    return (lax.axis_index("latent") >> 1) ^ r


def block_rows(r):
    return pl.ds(pl.multiple_of(block_of(r) * BLOCK, BLOCK), BLOCK)


def split_sum(rows):
    return rows[:8].astype(f32) + rows[8:].astype(f32)


def split(value):
    high = value.astype(bf16)
    low = (value - high.astype(f32)).astype(bf16)
    return jnp.concatenate([high, low], axis=0)


def product(rows, weights):
    return lax.dot_general(rows, weights, NT, preferred_element_type=f32).astype(bf16)


def encode_first(acts, weights, blocks):
    def kernel(a, w, *refs):
        rows, held, sem, w_sem = refs[-4:]
        latent = lax.axis_index("latent")
        copies = []
        for k in range(4):
            at = ((latent & 1) ^ (k // 2)) * HALF + ((latent >> 3) ^ (k % 2)) * QUARTER
            source = a.at[pl.ds(pl.multiple_of(at, QUARTER), QUARTER)]
            target = rows.at[pl.ds(k * QUARTER, QUARTER)]
            copies.append(pltpu.make_async_copy(source, target, sem.at[k]))
        w_copies = [
            pltpu.make_async_copy(w.at[block_rows(r)], held.at[k], w_sem.at[k])
            for k, r in enumerate(blocks)
        ]
        for copy in copies + w_copies:
            copy.start()
        for copy in copies:
            copy.wait()
        for k in range(len(blocks)):
            w_copies[k].wait()
            refs[k][...] = product(rows[...], held[k])

    return call(
        kernel,
        (acts, weights),
        [half(ROWS, BLOCK)] * len(blocks) + [half(ROWS, D)],
        "encode_first",
        MATMUL * len(blocks) // LAYERS,
        [
            pltpu.VMEM((len(blocks), BLOCK, D), bf16),
            pltpu.SemaphoreType.DMA((4,)),
            pltpu.SemaphoreType.DMA((len(blocks),)),
        ],
        51,
        [HBM, HBM],
    )


def encode(rows, weights, blocks):
    def kernel(a, w, *outs):
        for out, r in zip(outs, blocks):
            out[...] = product(a[...], w[block_rows(r)])

    return call(
        kernel,
        (rows, weights),
        [half(ROWS, BLOCK)] * len(blocks),
        "encode",
        MATMUL * len(blocks) // LAYERS,
        mib=8,
    )


def prepare(rows, weights):
    def kernel(a, w, norms, piece, held):
        for r in range(LAYERS):
            wb = w[block_rows(r)]
            squares = jnp.zeros((BLOCK, 128), f32)
            for i in range(D // 128):
                x = wb[:, i * 128 : (i + 1) * 128].astype(f32)
                squares = squares + x * x
            total = lax.dot_general(
                jnp.ones((8, 128), f32),
                squares,
                NT,
                precision=lax.Precision.HIGHEST,
                preferred_element_type=f32,
            )
            norms[r] = jnp.sqrt(total + norm_eps)
        value = a[:QUARTER].astype(f32)
        for k in range(4):
            held[k] = value[k * PIECE : (k + 1) * PIECE]
        piece[...] = held[chip_of(0) & 3].astype(bf16)

    return call(
        kernel,
        (rows, weights),
        [full(LAYERS, 8, BLOCK), half(PIECE, D)],
        "prepare",
        1 << 30,
        [pltpu.VMEM((4, PIECE, D), f32)],
        8,
    )


def add(terms):
    value = terms[0][:ROWS].astype(f32)
    for x in terms[1:]:
        value = value + x[:ROWS].astype(f32)
    return value


def add_extra(terms):
    return sum(split_sum(x[ROWS:]) for x in terms)


def add_z(terms):
    extra = terms[0].shape[0] - ROWS

    def kernel(*refs):
        *t, out = refs
        out[:ROWS] = add(t).astype(bf16)
        if extra:
            out[ROWS:] = split(add_extra(t))

    return call(kernel, terms, half(*terms[0].shape), "add_z", 1 << 20)


def activate(terms, bias):
    def kernel(*refs):
        t, (b, out) = refs[:5], refs[5:]
        out[...] = jnp.maximum(add(t) + b[block_of(0)], 0.0).astype(bf16)

    return call(kernel, (*terms, bias), half(ROWS, BLOCK), "activate", 1 << 20)


def decode(active, weights, blocks, before, last):
    width = 768
    count = len(blocks)

    def kernel(*refs):
        g, w = refs[:count], refs[count]
        lat, *outs = refs[count + 1 + len(before) :]
        for k in range(count):
            x = g[k][...].astype(f32)
            lat[k] = (x * x).astype(bf16)
        for i in range(D // width):
            cols = slice(i * width, (i + 1) * width)
            value = refs[count + 1][:, cols] if before else None
            for k, r in enumerate(blocks):
                term = jnp.dot(lat[k], w[block_rows(r), cols], preferred_element_type=f32)
                value = term if value is None else value + term
            if last:
                for k in range(4):
                    outs[k][:, cols] = value[k * QUARTER : (k + 1) * QUARTER].astype(bf16)
            else:
                outs[0][:, cols] = value

    return call(
        kernel,
        (*active, weights, *before),
        [half(count, ROWS, BLOCK)] + ([half(QUARTER, D)] * 4 if last else [full(ROWS, D)]),
        "decode",
        MATMUL * count // LAYERS,
        mib=12,
    )


def latents_of(lats, r):
    for lat, blocks in zip(lats, BACK):
        if r in blocks:
            return lat[blocks.index(r)]


def add_core(own, other):
    def kernel(a, b, *refs):
        outs, held = refs[:4], refs[4]
        total = a[...].astype(f32) + b[...].astype(f32)
        for k in range(4):
            held[k] = total[k * PIECE : (k + 1) * PIECE]
        for k in range(4):
            outs[k][...] = held[chip_of(k) & 3].astype(bf16)

    return call(
        kernel,
        (own, other),
        [half(PIECE, D)] * 4,
        "add_core",
        1 << 20,
        [pltpu.VMEM((4, PIECE, D), f32)],
    )


def add_x(terms):
    def kernel(*refs):
        *t, out = refs
        value = t[0][...].astype(f32)
        for x in t[1:]:
            value = value + x[...].astype(f32)
        out[...] = value.astype(bf16)

    return call(kernel, terms, half(PIECE, D), "add_x", 1 << 20)


def error(terms, bias, acts):
    def kernel(*refs):
        t, (b, x, out) = refs[:5], refs[5:]
        value = t[0][...].astype(f32)
        for y in t[1:]:
            value = value + y[...].astype(f32)
        out[...] = ((value + b[...] - x[...].astype(f32)) * (2.0 / ROWS)).astype(bf16)

    return call(kernel, (*terms, bias, acts), half(PIECE, D), "error", 1 << 20)


def join(parts):
    def kernel(*refs):
        out, held = refs[4:]
        for k in range(4):
            held[chip_of(k) & 3] = refs[k][...].astype(f32)
        out[...] = jnp.concatenate([held[k] for k in range(4)], axis=0).astype(bf16)

    return call(
        kernel,
        parts,
        half(4 * PIECE, D),
        "join",
        1 << 20,
        [pltpu.VMEM((4, PIECE, D), f32)],
    )


def backward_first(parts, rows, norms, weights, blocks):
    count = len(blocks)

    def kernel(*refs):
        p, (x, n, w), outs, both = refs[:4], refs[4:7], refs[7 : 7 + count], refs[7 + count]
        for k in range(4):
            both[k * QUARTER : (k + 1) * QUARTER] = p[k][...]
        for out, r in zip(outs, blocks):
            out[:ROWS] = product(both[:ROWS], w[block_rows(r)])
            out[ROWS:] = split(n[r])
        both[ROWS:] = x[...]

    return call(
        kernel,
        (*parts, rows, norms, weights),
        [half(ROWS + EXTRA, BLOCK)] * count + [half(2 * ROWS, D)],
        "backward_first",
        MATMUL * count // LAYERS,
        mib=8,
    )


def backward(both, norms, weights, blocks):
    def kernel(e, n, w, *outs):
        for out, r in zip(outs, blocks):
            out[:ROWS] = product(e[:ROWS], w[block_rows(r)])
            out[ROWS:] = split(n[r])

    return call(
        kernel,
        (both, norms, weights),
        [half(ROWS + EXTRA, BLOCK)] * len(blocks),
        "backward",
        MATMUL * len(blocks) // LAYERS,
        mib=8,
    )


def latent_grad(terms, active, ready):
    def kernel(*refs):
        t, (a, _, out) = refs[:5], refs[5:]
        total = add_extra(t)
        value = add(t) + SCALE * total[:1]
        out[:ROWS] = (value * (2.0 * a[...].astype(f32))).astype(bf16)
        out[ROWS:] = split(total)

    return call(
        kernel,
        (*terms, active, ready),
        half(ROWS + EXTRA, BLOCK),
        "latent_grad",
        1 << 20,
        places=[VMEM] * 6 + [HBM],
    )


def prepare_gradient(lats, both, norms, weights):
    width = 768

    def kernel(*refs):
        ls, (e, n, w, out) = refs[: len(BACK)], refs[len(BACK) :]
        for k, r in enumerate(READY):
            l = latents_of(ls, r)
            column = penalty(l, n[r])
            for i in range(D // width):
                cols = slice(i * width, (i + 1) * width)
                g = lax.dot_general(l, e[:ROWS, cols], TN, preferred_element_type=f32)
                out[k, :, cols] = (g + column * w[block_rows(r), cols].astype(f32)).astype(bf16)

    return call(
        kernel,
        (*lats, both, norms, weights),
        half(len(READY), BLOCK, D),
        "prepare_gradient",
        MATMUL * len(READY) // LAYERS,
        mib=8,
    )


def penalty(lat, norms):
    usage = jnp.sum(lat.astype(f32), axis=0, keepdims=True)
    return (SCALE * jnp.broadcast_to(usage, (8, BLOCK)) / norms).T[:, :1]


def gradient(lats, dpres, both, norms, weights, ready, blocks, before=None, last=False):
    width = 768
    steps = D // width
    count = len(blocks)
    used = tuple(range(LAYERS)) if last else blocks
    first = before is None

    def kernel(*refs):
        ls, refs = refs[: len(BACK)], refs[len(BACK) :]
        d = dict(zip(used, refs))
        e, n, w, p = refs[len(used) : len(used) + 4]
        refs = refs[len(used) + 4 + (not first) :]
        out, lhs, buf, sem = refs[0], *refs[-3:]
        copies = []
        if first:
            bias, held, bias_sem = refs[1:4]
            held[...] = jnp.sum(e[:ROWS].astype(f32), axis=0, keepdims=True)
            copies.append(pltpu.make_async_copy(held, bias, bias_sem.at[0]))
        if last:
            enc, totals, held, sums, bias_sem = refs[1:6]
            for r in range(LAYERS):
                x = d[r][:ROWS].astype(f32)
                held[block_of(r)] = jnp.sum(x, axis=0, keepdims=True)
                sums[block_of(r)] = split_sum(d[r][ROWS:])[:1]
            copies.append(pltpu.make_async_copy(held, enc, bias_sem.at[0]))
            copies.append(pltpu.make_async_copy(sums, totals, bias_sem.at[1]))
        for copy in copies:
            copy.start()
        for k, r in enumerate(blocks):
            if r not in READY:
                l = latents_of(ls, r)
                lhs[:ROWS] = l
                lhs[ROWS:] = d[r][:ROWS]
                column = penalty(l, n[r])
            for i in range(steps):
                cols = slice(i * width, (i + 1) * width)
                if r in READY:
                    x = d[r][:ROWS]
                    g = lax.dot_general(x, e[ROWS:, cols], TN, preferred_element_type=f32)
                    g = g + p[READY.index(r), :, cols].astype(f32)
                else:
                    g = lax.dot_general(lhs[...], e[:, cols], TN, preferred_element_type=f32)
                    g = g + column * w[block_rows(r), cols].astype(f32)
                buf[k, :, cols] = g.astype(bf16)
                copy = pltpu.make_async_copy(
                    buf.at[k, :, cols], out.at[block_rows(r), cols], sem.at[k, i]
                )
                copy.start()
                copies.append(copy)
        for copy in copies:
            copy.wait()

    shapes, scratch = [half(F, D)], []
    if first:
        shapes.append(full(1, D))
        scratch += [pltpu.VMEM((1, D), f32), pltpu.SemaphoreType.DMA((1,))]
    if last:
        shapes += [full(LAYERS, 1, BLOCK)] * 2
        scratch += [pltpu.VMEM((LAYERS, 1, BLOCK), f32)] * 2 + [pltpu.SemaphoreType.DMA((2,))]
    operands = (*lats, *[dpres[r] for r in used], both, norms, weights, ready)
    return call(
        kernel,
        operands if first else (*operands, before),
        shapes,
        "gradient",
        2 * MATMUL * count // LAYERS,
        scratch
        + [
            pltpu.VMEM((2 * ROWS, BLOCK), bf16),
            pltpu.VMEM((count, BLOCK, D), bf16),
            pltpu.SemaphoreType.DMA((count, steps)),
        ],
        12,
        [VMEM] * len(operands) + ([] if first else [HBM]),
        [HBM] * len(shapes),
        None if first else {len(operands): 0},
    )


def scatter(terms, ring, pair, add):
    cross = pair(terms[6])
    far = [ring(terms[4 + d], d) for d in SIDES]
    near = [ring(terms[d], d) for d in SIDES]
    other = pair(add([terms[4]] + far))
    return [terms[0]] + near + [ring(add([terms[2], cross]), 2), other]


def gather(own, ring, pair):
    blocks = {0: own, 4: pair(own), 2: ring(own, 2)}
    for r in (0, 4):
        for d in SIDES:
            blocks[r + d] = ring(blocks[r], d)
    blocks[6] = pair(blocks[2])
    return blocks


def body(acts, decoder, enc_bias, dec_bias):
    inputs, weights = acts[0], decoder[0]
    bias = enc_bias.reshape(LAYERS, 1, BLOCK)

    *out, rows = encode_first(inputs, weights, SENT[0])
    for blocks in SENT[1:]:
        out += encode(rows, weights, blocks)
    terms = dict(zip(sum(SENT, ()), out))
    norms, piece = prepare(rows, weights)
    mine = activate(scatter(terms, move_z, move_y, add_z), bias)
    active = gather(mine, move_z, move_y)
    lats, before = [], ()
    for blocks in BACK:
        last = blocks is BACK[-1]
        lat, *before = decode([active[r] for r in blocks], weights, blocks, before, last)
        lats.append(lat)

    far, near = [add_core(before[k], move_core(before[2 + k])) for k in (1, 0)]
    own = error(scatter([*near, *far], move_x, move_lo, add_x), dec_bias, piece)
    got = gather(own, move_x, move_lo)
    errors = [join([got[r + k] for k in range(4)]) for r in (0, 4)]
    errors += [move_core(x) for x in errors]

    *out, both = backward_first(errors, rows, norms, weights, SENT[0])
    for blocks in SENT[1:]:
        out += backward(both, norms, weights, blocks)
    terms = dict(zip(sum(SENT, ()), out))
    ready = prepare_gradient(lats, both, norms, weights)
    dpre = latent_grad(scatter(terms, move_z, move_y, add_z), mine, ready)
    dpres = gather(dpre, move_z, move_y)
    grad = None
    for i, blocks in enumerate(GROUPS):
        last = i == len(GROUPS) - 1
        out = gradient(lats, dpres, both, norms, weights, ready, blocks, grad, last)
        grad = out[0]
        if i == 0:
            dec_grad = out[1]
    enc_grad, total = out[1:]
    return grad[None], enc_grad.reshape(F), dec_grad, total.reshape(F)


def solution(mesh):
    placed = (P("layer", None, None), P("layer", "latent", None), P("latent"), P("layer", None))
    return jax.shard_map(
        body,
        mesh=mesh,
        in_specs=placed,
        out_specs=(P("layer", "latent", None), P("latent"), P("layer", None), P("latent")),
        check_vma=False,
    )
```

```python
import jax
import jax.numpy as jnp
from jax import lax
from jax.experimental import pallas as pl
from jax.experimental.pallas import tpu as pltpu
from jax.sharding import PartitionSpec as P

penalty_weight = 3.0
norm_eps = 1e-06

D = 2304
ROWS = 384
HALF = ROWS // 2
F = 2048
LAYERS = 8
BLOCK = F // LAYERS
CHIPS = 8
QUARTER = HALF // 2
PIECE = HALF // CHIPS
EXTRA = 16
GROUPS = ((0,), (4, 2, 1, 3), (5, 7, 6))
READY = (1, 2, 3, 4, 5, 6, 7)
SENT = ((5, 7, 6), (1, 3), (4, 0, 2))
BACK = ((0, 1, 2, 3), (4, 5, 7), (6,))
SCALE = penalty_weight / ROWS
MATMUL = 2 * ROWS * F * D

SIDES = (1, 3)

f32 = jnp.float32
bf16 = jnp.bfloat16
NT = (((1,), (1,)), ((), ()))
TN = (((0,), (0,)), ((), ()))
VMEM = pl.BlockSpec(memory_space=pltpu.VMEM)
HBM = pl.BlockSpec(memory_space=pl.ANY)


def half(*shape):
    return jax.ShapeDtypeStruct(shape, bf16)


def full(*shape):
    return jax.ShapeDtypeStruct(shape, f32)


def call(kernel, operands, out_shape, name, flops, scratch=(), mib=4, places=None, outs=None, aliases=None):
    many = isinstance(out_shape, (list, tuple))
    return pl.pallas_call(
        kernel,
        in_specs=places or [VMEM] * len(operands),
        out_specs=outs or ([VMEM] * len(out_shape) if many else VMEM),
        out_shape=out_shape,
        scratch_shapes=list(scratch),
        input_output_aliases=aliases or {},
        compiler_params=pltpu.CompilerParams(vmem_limit_bytes=mib << 20),
        cost_estimate=pl.CostEstimate(flops=flops, bytes_accessed=flops // 400, transcendentals=0),
        name=name,
    )(*operands)


def move_y(x):
    return lax.ppermute(x, "layer", [(i, i ^ 4) for i in range(8)])


def move_z(x, r):
    return lax.ppermute(x, "layer", [(i, i ^ r) for i in range(8)])


def move_core(x):
    return lax.ppermute(x, "latent", [(i, i ^ 1) for i in range(16)])


def move_lo(x):
    return lax.ppermute(x, "latent", [(i, i ^ 8) for i in range(16)])


def move_x(x, r):
    return lax.ppermute(x, "latent", [(i, i ^ (2 * r)) for i in range(16)])


def block_of(r):
    return lax.axis_index("layer") ^ r


def chip_of(r):
    return (lax.axis_index("latent") >> 1) ^ r


def block_rows(r):
    return pl.ds(pl.multiple_of(block_of(r) * BLOCK, BLOCK), BLOCK)


def split_sum(rows):
    return rows[:8].astype(f32) + rows[8:].astype(f32)


def split(value):
    high = value.astype(bf16)
    low = (value - high.astype(f32)).astype(bf16)
    return jnp.concatenate([high, low], axis=0)


def product(rows, weights):
    return lax.dot_general(rows, weights, NT, preferred_element_type=f32).astype(bf16)


def encode_first(acts, weights, blocks):
    def kernel(a, w, *refs):
        rows, held, sem, w_sem = refs[-4:]
        latent = lax.axis_index("latent")
        copies = []
        for k in range(4):
            at = ((latent & 1) ^ (k // 2)) * HALF + ((latent >> 3) ^ (k % 2)) * QUARTER
            source = a.at[pl.ds(pl.multiple_of(at, QUARTER), QUARTER)]
            target = rows.at[pl.ds(k * QUARTER, QUARTER)]
            copies.append(pltpu.make_async_copy(source, target, sem.at[k]))
        w_copies = [
            pltpu.make_async_copy(w.at[block_rows(r)], held.at[k], w_sem.at[k])
            for k, r in enumerate(blocks)
        ]
        for copy in w_copies[:1] + copies + w_copies[1:]:
            copy.start()
        for copy in copies:
            copy.wait()
        for k in range(len(blocks)):
            w_copies[k].wait()
            refs[k][...] = product(rows[...], held[k])

    return call(
        kernel,
        (acts, weights),
        [half(ROWS, BLOCK)] * len(blocks) + [half(ROWS, D)],
        "encode_first",
        MATMUL * len(blocks) // LAYERS,
        [
            pltpu.VMEM((len(blocks), BLOCK, D), bf16),
            pltpu.SemaphoreType.DMA((4,)),
            pltpu.SemaphoreType.DMA((len(blocks),)),
        ],
        51,
        [HBM, HBM],
    )


def encode(rows, weights, blocks):
    def kernel(a, w, *outs):
        for out, r in zip(outs, blocks):
            out[...] = product(a[...], w[block_rows(r)])

    return call(
        kernel,
        (rows, weights),
        [half(ROWS, BLOCK)] * len(blocks),
        "encode",
        MATMUL * len(blocks) // LAYERS,
        mib=8,
    )


def prepare(rows, weights):
    def kernel(a, w, norms, piece, held):
        for r in range(LAYERS):
            wb = w[block_rows(r)]
            squares = jnp.zeros((BLOCK, 128), f32)
            for i in range(D // 128):
                x = wb[:, i * 128 : (i + 1) * 128].astype(f32)
                squares = squares + x * x
            total = lax.dot_general(
                jnp.ones((8, 128), f32),
                squares,
                NT,
                precision=lax.Precision.HIGHEST,
                preferred_element_type=f32,
            )
            norms[r] = jnp.sqrt(total + norm_eps)
        value = a[:QUARTER].astype(f32)
        for k in range(4):
            held[k] = value[k * PIECE : (k + 1) * PIECE]
        piece[...] = held[chip_of(0) & 3].astype(bf16)

    return call(
        kernel,
        (rows, weights),
        [full(LAYERS, 8, BLOCK), half(PIECE, D)],
        "prepare",
        1 << 30,
        [pltpu.VMEM((4, PIECE, D), f32)],
        8,
    )


def add(terms):
    value = terms[0][:ROWS].astype(f32)
    for x in terms[1:]:
        value = value + x[:ROWS].astype(f32)
    return value


def add_extra(terms):
    return sum(split_sum(x[ROWS:]) for x in terms)


def add_z(terms):
    extra = terms[0].shape[0] - ROWS

    def kernel(*refs):
        *t, out = refs
        out[:ROWS] = add(t).astype(bf16)
        if extra:
            out[ROWS:] = split(add_extra(t))

    return call(kernel, terms, half(*terms[0].shape), "add_z", 1 << 20)


def activate(terms, bias):
    def kernel(*refs):
        t, (b, out) = refs[:5], refs[5:]
        out[...] = jnp.maximum(add(t) + b[block_of(0)], 0.0).astype(bf16)

    return call(kernel, (*terms, bias), half(ROWS, BLOCK), "activate", 1 << 20)


def decode(active, weights, blocks, before, last):
    width = 768
    count = len(blocks)

    def kernel(*refs):
        g, w = refs[:count], refs[count]
        lat, *outs = refs[count + 1 + len(before) :]
        for k in range(count):
            x = g[k][...].astype(f32)
            lat[k] = (x * x).astype(bf16)
        for i in range(D // width):
            cols = slice(i * width, (i + 1) * width)
            value = refs[count + 1][:, cols] if before else None
            for k, r in enumerate(blocks):
                term = jnp.dot(lat[k], w[block_rows(r), cols], preferred_element_type=f32)
                value = term if value is None else value + term
            if last:
                for k in range(4):
                    outs[k][:, cols] = value[k * QUARTER : (k + 1) * QUARTER].astype(bf16)
            else:
                outs[0][:, cols] = value

    return call(
        kernel,
        (*active, weights, *before),
        [half(count, ROWS, BLOCK)] + ([half(QUARTER, D)] * 4 if last else [full(ROWS, D)]),
        "decode",
        MATMUL * count // LAYERS,
        mib=12,
    )


def latents_of(lats, r):
    for lat, blocks in zip(lats, BACK):
        if r in blocks:
            return lat[blocks.index(r)]


def add_core(own, other):
    def kernel(a, b, *refs):
        outs, held = refs[:4], refs[4]
        total = a[...].astype(f32) + b[...].astype(f32)
        for k in range(4):
            held[k] = total[k * PIECE : (k + 1) * PIECE]
        for k in range(4):
            outs[k][...] = held[chip_of(k) & 3].astype(bf16)

    return call(
        kernel,
        (own, other),
        [half(PIECE, D)] * 4,
        "add_core",
        1 << 20,
        [pltpu.VMEM((4, PIECE, D), f32)],
    )


def add_x(terms):
    def kernel(*refs):
        *t, out = refs
        value = t[0][...].astype(f32)
        for x in t[1:]:
            value = value + x[...].astype(f32)
        out[...] = value.astype(bf16)

    return call(kernel, terms, half(PIECE, D), "add_x", 1 << 20)


def error(terms, bias, acts):
    def kernel(*refs):
        t, (b, x, out) = refs[:5], refs[5:]
        value = t[0][...].astype(f32)
        for y in t[1:]:
            value = value + y[...].astype(f32)
        out[...] = ((value + b[...] - x[...].astype(f32)) * (2.0 / ROWS)).astype(bf16)

    return call(kernel, (*terms, bias, acts), half(PIECE, D), "error", 1 << 20)


def join(parts):
    def kernel(*refs):
        out, held = refs[4:]
        for k in range(4):
            held[chip_of(k) & 3] = refs[k][...].astype(f32)
        out[...] = jnp.concatenate([held[k] for k in range(4)], axis=0).astype(bf16)

    return call(
        kernel,
        parts,
        half(4 * PIECE, D),
        "join",
        1 << 20,
        [pltpu.VMEM((4, PIECE, D), f32)],
    )


def backward_first(parts, rows, norms, weights, blocks):
    count = len(blocks)

    def kernel(*refs):
        p, (x, n, w), outs, both = refs[:4], refs[4:7], refs[7 : 7 + count], refs[7 + count]
        for k in range(4):
            both[k * QUARTER : (k + 1) * QUARTER] = p[k][...]
        for out, r in zip(outs, blocks):
            out[:ROWS] = product(both[:ROWS], w[block_rows(r)])
            out[ROWS:] = split(n[r])
        both[ROWS:] = x[...]

    return call(
        kernel,
        (*parts, rows, norms, weights),
        [half(ROWS + EXTRA, BLOCK)] * count + [half(2 * ROWS, D)],
        "backward_first",
        MATMUL * count // LAYERS,
        mib=8,
    )


def backward(both, norms, weights, blocks):
    def kernel(e, n, w, *outs):
        for out, r in zip(outs, blocks):
            out[:ROWS] = product(e[:ROWS], w[block_rows(r)])
            out[ROWS:] = split(n[r])

    return call(
        kernel,
        (both, norms, weights),
        [half(ROWS + EXTRA, BLOCK)] * len(blocks),
        "backward",
        MATMUL * len(blocks) // LAYERS,
        mib=8,
    )


def latent_grad(terms, active, ready):
    def kernel(*refs):
        t, (a, _, out) = refs[:5], refs[5:]
        total = add_extra(t)
        value = add(t) + SCALE * total[:1]
        out[:ROWS] = (value * (2.0 * a[...].astype(f32))).astype(bf16)
        out[ROWS:] = split(total)

    return call(
        kernel,
        (*terms, active, ready),
        half(ROWS + EXTRA, BLOCK),
        "latent_grad",
        1 << 20,
        places=[VMEM] * 6 + [HBM],
    )


def prepare_gradient(lats, both, norms, weights):
    width = 768

    def kernel(*refs):
        ls, (e, n, w, out) = refs[: len(BACK)], refs[len(BACK) :]
        for k, r in enumerate(READY):
            l = latents_of(ls, r)
            column = penalty(l, n[r])
            for i in range(D // width):
                cols = slice(i * width, (i + 1) * width)
                g = lax.dot_general(l, e[:ROWS, cols], TN, preferred_element_type=f32)
                out[k, :, cols] = (g + column * w[block_rows(r), cols].astype(f32)).astype(bf16)

    return call(
        kernel,
        (*lats, both, norms, weights),
        half(len(READY), BLOCK, D),
        "prepare_gradient",
        MATMUL * len(READY) // LAYERS,
        mib=8,
    )


def penalty(lat, norms):
    usage = jnp.sum(lat.astype(f32), axis=0, keepdims=True)
    return (SCALE * jnp.broadcast_to(usage, (8, BLOCK)) / norms).T[:, :1]


def gradient(lats, dpres, both, norms, weights, ready, blocks, before=None, last=False):
    width = 768
    steps = D // width
    count = len(blocks)
    used = tuple(range(LAYERS)) if last else blocks
    first = before is None

    def kernel(*refs):
        ls, refs = refs[: len(BACK)], refs[len(BACK) :]
        d = dict(zip(used, refs))
        e, n, w, p = refs[len(used) : len(used) + 4]
        refs = refs[len(used) + 4 + (not first) :]
        out, lhs, buf, sem = refs[0], *refs[-3:]
        copies = []
        if first:
            bias, held, bias_sem = refs[1:4]
            held[...] = jnp.sum(e[:ROWS].astype(f32), axis=0, keepdims=True)
            copies.append(pltpu.make_async_copy(held, bias, bias_sem.at[0]))
        if last:
            enc, totals, held, sums, bias_sem = refs[1:6]
            for r in range(LAYERS):
                x = d[r][:ROWS].astype(f32)
                held[block_of(r)] = jnp.sum(x, axis=0, keepdims=True)
                sums[block_of(r)] = split_sum(d[r][ROWS:])[:1]
            copies.append(pltpu.make_async_copy(held, enc, bias_sem.at[0]))
            copies.append(pltpu.make_async_copy(sums, totals, bias_sem.at[1]))
        for copy in copies:
            copy.start()
        for k, r in enumerate(blocks):
            if r not in READY:
                l = latents_of(ls, r)
                lhs[:ROWS] = l
                lhs[ROWS:] = d[r][:ROWS]
                column = penalty(l, n[r])
            for i in range(steps):
                cols = slice(i * width, (i + 1) * width)
                if r in READY:
                    x = d[r][:ROWS]
                    g = lax.dot_general(x, e[ROWS:, cols], TN, preferred_element_type=f32)
                    g = g + p[READY.index(r), :, cols].astype(f32)
                else:
                    g = lax.dot_general(lhs[...], e[:, cols], TN, preferred_element_type=f32)
                    g = g + column * w[block_rows(r), cols].astype(f32)
                buf[k, :, cols] = g.astype(bf16)
                copy = pltpu.make_async_copy(
                    buf.at[k, :, cols], out.at[block_rows(r), cols], sem.at[k, i]
                )
                copy.start()
                copies.append(copy)
        for copy in copies:
            copy.wait()

    shapes, scratch = [half(F, D)], []
    if first:
        shapes.append(full(1, D))
        scratch += [pltpu.VMEM((1, D), f32), pltpu.SemaphoreType.DMA((1,))]
    if last:
        shapes += [full(LAYERS, 1, BLOCK)] * 2
        scratch += [pltpu.VMEM((LAYERS, 1, BLOCK), f32)] * 2 + [pltpu.SemaphoreType.DMA((2,))]
    operands = (*lats, *[dpres[r] for r in used], both, norms, weights, ready)
    return call(
        kernel,
        operands if first else (*operands, before),
        shapes,
        "gradient",
        2 * MATMUL * count // LAYERS,
        scratch
        + [
            pltpu.VMEM((2 * ROWS, BLOCK), bf16),
            pltpu.VMEM((count, BLOCK, D), bf16),
            pltpu.SemaphoreType.DMA((count, steps)),
        ],
        12,
        [VMEM] * len(operands) + ([] if first else [HBM]),
        [HBM] * len(shapes),
        None if first else {len(operands): 0},
    )


def scatter(terms, ring, pair, add):
    cross = pair(terms[6])
    far = [ring(terms[4 + d], d) for d in SIDES]
    near = [ring(terms[d], d) for d in SIDES]
    other = pair(add([terms[4]] + far))
    return [terms[0]] + near + [ring(add([terms[2], cross]), 2), other]


def gather(own, ring, pair):
    blocks = {0: own, 4: pair(own), 2: ring(own, 2)}
    for r in (0, 4):
        for d in SIDES:
            blocks[r + d] = ring(blocks[r], d)
    blocks[6] = pair(blocks[2])
    return blocks


def body(acts, decoder, enc_bias, dec_bias):
    inputs, weights = acts[0], decoder[0]
    bias = enc_bias.reshape(LAYERS, 1, BLOCK)

    *out, rows = encode_first(inputs, weights, SENT[0])
    for blocks in SENT[1:]:
        out += encode(rows, weights, blocks)
    terms = dict(zip(sum(SENT, ()), out))
    norms, piece = prepare(rows, weights)
    mine = activate(scatter(terms, move_z, move_y, add_z), bias)
    active = gather(mine, move_z, move_y)
    lats, before = [], ()
    for blocks in BACK:
        last = blocks is BACK[-1]
        lat, *before = decode([active[r] for r in blocks], weights, blocks, before, last)
        lats.append(lat)

    far, near = [add_core(before[k], move_core(before[2 + k])) for k in (1, 0)]
    own = error(scatter([*near, *far], move_x, move_lo, add_x), dec_bias, piece)
    got = gather(own, move_x, move_lo)
    errors = [join([got[r + k] for k in range(4)]) for r in (0, 4)]
    errors += [move_core(x) for x in errors]

    *out, both = backward_first(errors, rows, norms, weights, SENT[0])
    for blocks in SENT[1:]:
        out += backward(both, norms, weights, blocks)
    terms = dict(zip(sum(SENT, ()), out))
    ready = prepare_gradient(lats, both, norms, weights)
    dpre = latent_grad(scatter(terms, move_z, move_y, add_z), mine, ready)
    dpres = gather(dpre, move_z, move_y)
    grad = None
    for i, blocks in enumerate(GROUPS):
        last = i == len(GROUPS) - 1
        out = gradient(lats, dpres, both, norms, weights, ready, blocks, grad, last)
        grad = out[0]
        if i == 0:
            dec_grad = out[1]
    enc_grad, total = out[1:]
    return grad[None], enc_grad.reshape(F), dec_grad, total.reshape(F)


def solution(mesh):
    placed = (P("layer", None, None), P("layer", "latent", None), P("latent"), P("layer", None))
    return jax.shard_map(
        body,
        mesh=mesh,
        in_specs=placed,
        out_specs=(P("layer", "latent", None), P("latent"), P("layer", None), P("latent")),
        check_vma=False,
    )
```
